32 devices in a mesh: dp: 8 (over z, y), tensor: 4 (over x, core).
Axes of the slice: x: 2, y: 2, z: 4, core: 2. Of those that a mesh axis runs over, the one named last changes fastest.
Arguments:
- gene_ids: int32 [16384], P('dp'), may hold values from 0 to 35999
- know_ids: int32 [5, 16384], P(None, 'dp'), may hold values from 0 to 1023
- lengths: int32 [8], P('dp'), may hold values from 1 to 2048, as said below
- tables: bfloat16 [41120, 768], P('dp', 'tensor'), may hold values from -6 to 6
- norm_gain: bfloat16 [2, 768], replicated, may hold values from 0.5 to 1.5
- norm_bias: bfloat16 [2, 768], replicated, may hold values from -4 to 4
- qkv_weight: bfloat16 [3, 768, 768], P(None, None, 'tensor'), may hold values from -0.21875 to 0.21875
- qv_bias: bfloat16 [2, 768], P(None, 'tensor'), may hold values from -0.75 to 0.75
- out_weight: bfloat16 [768, 768], P('tensor'), may hold values from -1.75 to 1.75
- out_bias: bfloat16 [768], replicated, may hold values from -4 to 4
- up_weight: bfloat16 [768, 3072], P(None, 'tensor'), may hold values from -0.21875 to 0.21875
- up_bias: bfloat16 [3072], P('tensor'), may hold values from -6 to 6
- down_weight: bfloat16 [3072, 768], P('tensor'), may hold values from -0.109375 to 0.109375
- down_bias: bfloat16 [768], replicated, may hold values from -4 to 4
- cotangent: bfloat16 [16384, 768], P('dp'), may hold values from -6 to 6
Outputs:
- out: bfloat16 [16384, 768], P('dp')
- input_grad: float32 [16384, 768], P('dp')
- tables_grad: float32 [41120, 768], P('dp', 'tensor')
- norm_gain_grad: float32 [2, 768], replicated
- norm_bias_grad: float32 [2, 768], replicated
- qkv_grad: float32 [3, 768, 768], P(None, None, 'tensor')
- qv_bias_grad: float32 [2, 768], P(None, 'tensor')
- out_weight_grad: float32 [768, 768], P('tensor')
- out_bias_grad: float32 [768], replicated
- up_weight_grad: float32 [768, 3072], P(None, 'tensor')
- up_bias_grad: float32 [3072], P('tensor')
- down_weight_grad: float32 [3072, 768], P('tensor')
- down_bias_grad: float32 [768], replicated
The draws below stay inside these ranges and needn't reach their ends.
Inputs may be any that keep to these rules, and one draw needn't show every extreme that they name: `lengths`: every cell has at least one gene, and some cell has exactly 2048.
All inputs are finite; a program needn't handle non-finite values.
Results may differ from the reference program's by a relative error of at most 0.012.
The reference program's roundings to bfloat16 on the way count: a program that leaves them out, or rounds other values in their place, can miss the bound.
Values may be sent and summed in bfloat16 or wider, within the bound.
No kernel may reach another device: no remote copies, remote signals or barrier semaphores. Data moves between devices by JAX's collectives and lax.ppermute only.
A program may use at most 256 MiB of HBM per device.

```python
import math
import jax
import jax.numpy as jnp
import numpy as np
from jax import lax

D = 768
HEADS = 12
FF = 3072
VOCAB = 36000
KNOW = 1024
LEN = 2048
ROWS = 41120
CELLS = 8
TOKENS = 16384


def draw_lengths(key, part):
    key_bucket, key_jitter, key_full = jax.random.split(key, 3)
    bucket = jax.random.randint(key_bucket, (CELLS,), 1, 4)
    jitter = jax.random.randint(key_jitter, (CELLS,), 0, LEN // 8)
    drawn = LEN // bucket - jitter
    longest = jax.random.randint(key_full, (), 0, CELLS)
    return jnp.where(jnp.arange(CELLS) == longest, LEN, drawn).astype(jnp.int32)


def set_ends(values, key, low, high):
    longest = values.shape.index(max(values.shape))
    spots = []
    for shift in (0, 1):
        where = [jax.random.randint(jax.random.fold_in(key, axis), (), 0, length) for axis, length in enumerate(values.shape)]
        where[longest] = (where[longest] + shift) % values.shape[longest]
        spots.append(tuple(where))
    return values.at[spots[0]].set(low).at[spots[1]].set(high)


def level_of(stream_key, shape, shards, least, largest):
    def one(position, blocks):
        steps = jax.random.uniform(jax.random.fold_in(jax.random.fold_in(stream_key, 6), position), (blocks,), jnp.float32, least / len(shards), largest / len(shards))
        return jnp.repeat(jnp.exp(steps), shape[position] // blocks).reshape((-1,) + (1,) * (len(shape) - position - 1))

    level = one(*shards[0])
    for cut in shards[1:]:
        level = level * one(*cut)
    return level


def rank_table(count, skew):
    weights = [(1 << 20) // math.isqrt(grade ** skew) + 1 for grade in range(1, count + 1)]
    scale = 1 + sum(weights) // (1 << 30)
    return np.cumsum(np.array([max(1, weight // scale) for weight in weights]))


def skewed_ids(rng, shape, amount, skew):
    table = rank_table(amount, skew)
    pick = jax.random.randint(jax.random.fold_in(rng, 1), shape, 0, int(table[amount - 1]))
    standing = jnp.searchsorted(jnp.asarray(table, jnp.int32), pick, side="right")
    return jax.random.permutation(jax.random.fold_in(rng, 2), amount)[standing].astype(jnp.int32)


def normal_values(rng, dims, deviation, bound, cuts=(), kind=jnp.bfloat16):
    array = deviation * jax.random.normal(rng, dims, jnp.float32)
    if cuts:
        array = array * level_of(rng, dims, cuts, -0.22, 0.18)
    return jnp.clip(array, -bound, bound).astype(kind)


def setup_inputs(seed: int = 0) -> dict:
    key_of = jax.random.split(jax.random.key(seed), 16)
    return {
        "gene_ids": set_ends(skewed_ids(key_of[0], (TOKENS,), VOCAB, 1), jax.random.fold_in(key_of[0], 3), 0, VOCAB - 1).astype(jnp.int32),
        "know_ids": set_ends(jax.random.randint(key_of[1], (5, TOKENS), 0, KNOW), jax.random.fold_in(key_of[1], 1), 0, KNOW - 1).astype(jnp.int32),
        "lengths": draw_lengths(jax.random.fold_in(key_of[15], 71), 0),
        "tables": normal_values(key_of[3], (ROWS, D), 0.4, 6.0, ((0, 8), (1, 4))),
        "norm_gain": jnp.clip(1.0 + 0.1 * jax.random.normal(key_of[4], (2, D), jnp.float32), 0.5, 1.5).astype(jnp.bfloat16),
        "norm_bias": normal_values(key_of[5], (2, D), 0.3, 4.0),
        "qkv_weight": normal_values(key_of[6], (3, D, D), D ** -0.5, 0.21875, ((2, 4),)),
        "qv_bias": normal_values(key_of[7], (2, D), 0.05, 0.75, ((1, 4),)),
        "out_weight": normal_values(key_of[8], (D, D), (max(D // 64, 1)) ** -0.5, 1.75, ((0, 4),)),
        "out_bias": normal_values(key_of[9], (D,), 0.3, 4.0),
        "up_weight": normal_values(key_of[10], (D, FF), D ** -0.5, 0.21875, ((1, 4),)),
        "up_bias": normal_values(key_of[11], (FF,), 0.5, 6.0, ((0, 4),)),
        "down_weight": normal_values(key_of[12], (FF, D), FF ** -0.5, 0.109375, ((0, 4),)),
        "down_bias": normal_values(key_of[13], (D,), 0.3, 4.0),
        "cotangent": normal_values(key_of[14], (TOKENS, D), 1.0, 6.0, ((0, 8),)),
    }


@jax.custom_vjp
def low(v):
    return lax.optimization_barrier(v.astype(jnp.bfloat16)).astype(jnp.float32)

@jax.custom_vjp
def low_back(v):
    return v

def low_keep(v):
    return (low(v), None)

def low_pass(kept, grad):
    return (grad,)

def back_keep(v):
    return (v, None)

def back_low(kept, grad):
    return (low(grad),)
low.defvjp(low_keep, low_pass)
low_back.defvjp(back_keep, back_low)
norm_eps = 1e-05
highest = lax.Precision.HIGHEST

def matmul_high(left, right):
    return jnp.dot(left, right, precision=highest, preferred_element_type=jnp.float32)

def normalize(values, gain, shift):
    average = lax.optimization_barrier(jnp.mean(values, -1, keepdims=True))
    centered = values - average
    spread = lax.optimization_barrier(jnp.mean(centered * centered, -1, keepdims=True))
    return centered * lax.rsqrt(spread + norm_eps) * gain + shift

def attention(queries, keys, values, key_valid):
    length = queries.shape[0]
    block_rows = min(512, length)
    block_count = length // block_rows
    score_scale = queries.shape[2] ** (-0.5)

    def one_block(query_block):
        scores = jnp.einsum('qhd,khd->hqk', query_block, keys, precision=highest) * score_scale
        scores = jnp.where(key_valid[None, None, :], scores, -1e+30)
        scores = low_back(scores)
        probs = jax.nn.softmax(scores, axis=-1)
        return jnp.einsum('hqk,khd->qhd', low(probs), values, precision=highest)
    blocks = queries.reshape(block_count, block_rows, queries.shape[1], queries.shape[2])
    return lax.map(jax.checkpoint(one_block), blocks).reshape(length, -1)

def layer(embedded, weights, key_valid):
    norm_gain, norm_bias, qkv_weight, qv_bias, out_weight, out_bias, up_weight, up_bias, down_weight, down_bias = weights
    first = low(normalize(embedded, norm_gain[0], norm_bias[0]))
    query = low_back(low(matmul_high(first, qkv_weight[0]) + qv_bias[0]))
    key_rows = low_back(low(matmul_high(first, qkv_weight[1])))
    value = low_back(low(matmul_high(first, qkv_weight[2]) + qv_bias[1]))
    head_shape = (LEN, HEADS, D // HEADS)
    heads_out = attention(query.reshape(head_shape), key_rows.reshape(head_shape), value.reshape(head_shape), key_valid)
    heads_out = low_back(low(heads_out))
    resid = embedded + low_back(matmul_high(heads_out, out_weight)) + out_bias
    second = low(normalize(resid, norm_gain[1], norm_bias[1]))
    pre_act = low_back(matmul_high(second, up_weight) + up_bias)
    activated = low(jax.nn.gelu(pre_act, approximate=False))
    return resid + matmul_high(activated, down_weight) + down_bias

def reference(gene_ids, know_ids, lengths, tables, norm_gain, norm_bias, qkv_weight, qv_bias, out_weight, out_bias, up_weight, up_bias, down_weight, down_bias, cotangent):
    weights = tuple((w.astype(jnp.float32) for w in (norm_gain, norm_bias, qkv_weight, qv_bias, out_weight, out_bias, up_weight, up_bias, down_weight, down_bias)))
    table_float = tables.astype(jnp.float32)
    offsets = VOCAB + KNOW * jnp.arange(5, dtype=jnp.int32)[:, None]
    row_ids = jnp.concatenate([gene_ids[None, :].astype(jnp.int32), (know_ids + offsets).astype(jnp.int32)], 0)

    def embed(table):
        total = jnp.take(table, row_ids[0], axis=0)
        for index in range(1, 6):
            total = total + jnp.take(table, row_ids[index], axis=0)
        return total
    embedded, embed_back = jax.vjp(embed, table_float)
    key_valid = jnp.arange(LEN, dtype=jnp.int32)[None, :] < lengths[:, None]
    cell_inputs = embedded.reshape(CELLS, LEN, D)
    cell_cotangents = cotangent.reshape(CELLS, LEN, D)
    blank = jax.tree.map(jnp.zeros_like, weights)

    def one_cell(running, element):
        cell_input, cell_valid, cell_cotangent = element
        cell_out, cell_back = jax.vjp(lambda inputs, params: layer(inputs, params, cell_valid), cell_input, weights)
        grad_out = cell_cotangent.astype(jnp.float32) * cell_valid[:, None].astype(jnp.float32)
        grad_input, grad_weights = cell_back(grad_out)
        return (jax.tree.map(jnp.add, running, grad_weights), (cell_out.astype(jnp.bfloat16), grad_input))
    grads, (outputs, input_grads) = lax.scan(one_cell, blank, (cell_inputs, key_valid, cell_cotangents))
    input_grad = input_grads.reshape(TOKENS, D)
    tables_grad = embed_back(input_grad)[0]
    return (outputs.reshape(TOKENS, D), input_grad, tables_grad, grads[0], grads[1], grads[2], grads[3], grads[4], grads[5], grads[6], grads[7], grads[8], grads[9])
```

```python
from functools import partial

import jax
import jax.numpy as jnp
from jax import lax
from jax.experimental import pallas as pl
from jax.experimental.pallas import tpu as pltpu
from jax.sharding import PartitionSpec as P

HEADS = 12
VOCAB = 36000
KNOW = 1024
TABLES = 5
SHARDS = 8
norm_eps = 1e-05
BF = jnp.bfloat16
F32 = jnp.float32
I32 = jnp.int32
BIG = 56 * 1024 * 1024


def params():
    return pltpu.CompilerParams(vmem_limit_bytes=BIG)


def cost(micros):
    return pl.CostEstimate(
        flops=int(micros * 9e8), bytes_accessed=int(micros * 3e6), transcendentals=0
    )


def shape(dims, kind):
    return jax.ShapeDtypeStruct(dims, kind)


def dot_nt(left, right):
    return lax.dot_general(left, right, (((1,), (1,)), ((), ())), preferred_element_type=F32)


def dot_tn(left, right):
    return lax.dot_general(left, right, (((0,), (0,)), ((), ())), preferred_element_type=F32)


def dot_nn(left, right):
    return jnp.dot(left, right, preferred_element_type=F32)


def whole(dims):
    return pl.BlockSpec(dims, lambda i, *s: (0,) * len(dims))


def hot(condition):
    return condition.astype(F32).astype(BF)


def rows_like(dims):
    return lax.broadcasted_iota(I32, dims, 0)


def lanes_like(dims):
    return lax.broadcasted_iota(I32, dims, 1)


def after(value, *others):
    return lax.optimization_barrier((value, others))[0]


def hop(value, axis, flip):
    count = lax.axis_size(axis)
    return lax.ppermute(value, axis, [(i, i ^ flip) for i in range(count)])


def gather_four(block):
    far = hop(block, "tensor", 2)
    return [block, hop(block, "tensor", 1), far, hop(far, "tensor", 1)]


def swap_four(pieces):
    return [pieces[0]] + [hop(pieces[j], "tensor", j) for j in (1, 2, 3)]


def route_kernel(where_ref, ids_ref, lists_ref, slot_ref, most_ref, *, owned, slots):
    group, turn = where_ref[0], where_ref[1]
    ids = ids_ref[...]
    groups, count = ids.shape
    wanted = (ids >= group * owned) & (ids < (group + 1) * owned)
    mine = jnp.broadcast_to(ids[0:1, :], (groups, count))
    owners = rows_like((groups, count))
    held = (mine >= owners * owned) & (mine < (owners + 1) * owned)
    flags = jnp.concatenate([wanted.astype(F32), held.astype(F32)], 0)
    sums = flags
    lanes = lanes_like(flags.shape)
    step = 1
    while step < count:
        sums = sums + jnp.where(lanes >= step, pltpu.roll(sums, step, 1), 0.0)
        step *= 2
    low = (turn * slots).astype(F32)
    ranks = sums[:groups] - 1.0 - low
    ranks = jnp.where(wanted & (ranks >= 0.0) & (ranks < slots), ranks, -1.0).astype(I32)
    plus = jnp.where(wanted, ids - group * owned + 1, 0)
    spots = rows_like((slots, count))
    halves = rows_like((16, count))
    for k in range(groups):
        number = jnp.broadcast_to(plus[k : k + 1, :], (16, count))
        parts = jnp.where(halves == 0, number >> 8, jnp.where(halves == 1, number & 255, 0))
        parts = parts.astype(F32).astype(BF)
        match = hot(spots == ranks[k : k + 1, :])
        found = dot_nt(parts, match)
        lists_ref[group ^ k] = (found[0:1, :] * 256.0 + found[1:2, :]).astype(I32) - 1
    own = sums[groups:] - 1.0 - low
    good = held & (own >= 0.0) & (own < slots)
    slot = jnp.where(good, owners.astype(F32) * slots + own + 1.0, 0.0)
    slot = jnp.sum(slot, 0, keepdims=True) - 1.0
    slot_ref[...] = slot.astype(I32)
    most = jnp.zeros((groups, 1), F32)
    for o in range(groups):
        here = (ids >= o * owned) & (ids < (o + 1) * owned)
        most = jnp.maximum(most, jnp.sum(here.astype(F32), 1, keepdims=True))
    most_ref[...] = jnp.broadcast_to(jnp.max(most, 0, keepdims=True), (8, 128)).astype(I32)


def route(group, turn, ids, owned, slots):
    groups, count = ids.shape

    return pl.pallas_call(
        partial(route_kernel, owned=owned, slots=slots),
        grid_spec=pltpu.PrefetchScalarGridSpec(
            num_scalar_prefetch=1,
            grid=(1,),
            in_specs=[whole(ids.shape)],
            out_specs=[
                whole((groups, 1, slots)),
                whole((1, count)),
                whole((8, 128)),
            ],
        ),
        out_shape=[
            shape((groups, 1, slots), I32),
            shape((1, count), I32),
            shape((8, 128), I32),
        ],
        compiler_params=params(),
        cost_estimate=cost(8),
        name="route",
    )(jnp.stack([group, turn]), ids)


def pick_kernel(list_ref, table_ref, out_ref, *, chunk):
    wanted = list_ref[0]
    size = table_ref.shape[1]
    total = jnp.zeros(out_ref.shape[1:], F32)
    for start in range(0, size, chunk):
        part = min(chunk, size - start)
        match = hot(rows_like((part, wanted.shape[1])) == wanted - start)
        total += dot_nn(table_ref[:, start : start + part], match)
    out_ref[0] = total.astype(BF)


def pick(lists, table):
    groups, _, slots = lists.shape
    columns = table.shape[0]
    return pl.pallas_call(
        partial(pick_kernel, chunk=512),
        grid=(groups,),
        in_specs=[
            pl.BlockSpec((1, 1, slots), lambda i: (i, 0, 0)),
            pl.BlockSpec(table.shape, lambda i: (0, 0)),
        ],
        out_specs=pl.BlockSpec((1, columns, slots), lambda i: (i, 0, 0)),
        out_shape=shape((groups, columns, slots), BF),
        compiler_params=params(),
        cost_estimate=cost(12),
        name="pick",
    )(lists, table)


def embed_kernel(slot_ref, code_ref, moved_ref, know_ref, out_ref, table_ref):
    groups, columns, slots = moved_ref.shape
    shards, _, size = know_ref.shape

    @pl.when(pl.program_id(0) == 0)
    def _():
        for k in range(shards):
            table_ref[:, k * size : (k + 1) * size] = know_ref[k]

    slot = slot_ref[...]
    block = slot.shape[1]
    total = jnp.zeros((columns, block), F32)
    for n in range(groups):
        match = hot(rows_like((slots, block)) == slot - n * slots)
        total += dot_nn(moved_ref[n], match)
    for j in range(TABLES):
        match = hot(rows_like((KNOW, block)) == code_ref[j : j + 1, :])
        total += dot_nn(table_ref[:, j * KNOW : (j + 1) * KNOW], match)
    out_ref[...] = total.astype(BF)


def embed(slot, codes, moved, know):
    count = slot.shape[1]
    columns = moved.shape[1]
    block = min(512, count)
    return pl.pallas_call(
        embed_kernel,
        grid=(count // block,),
        in_specs=[
            pl.BlockSpec((1, block), lambda i: (0, i)),
            pl.BlockSpec((TABLES, block), lambda i: (0, i)),
            pl.BlockSpec(moved.shape, lambda i: (0, 0, 0)),
            pl.BlockSpec(know.shape, lambda i: (0, 0, 0)),
        ],
        out_specs=pl.BlockSpec((columns, block), lambda i: (0, i)),
        scratch_shapes=[pltpu.VMEM((columns, TABLES * KNOW), BF)],
        out_shape=shape((columns, count), BF),
        compiler_params=params(),
        cost_estimate=cost(13),
        name="embed",
    )(slot, codes, moved, know)


def more_kernel(slot_ref, moved_ref, have_ref, out_ref):
    groups, columns, slots = moved_ref.shape
    slot = slot_ref[...]
    block = slot.shape[1]
    total = have_ref[...].astype(F32)
    for n in range(groups):
        match = hot(rows_like((slots, block)) == slot - n * slots)
        total += dot_nn(moved_ref[n], match)
    out_ref[...] = total.astype(BF)


def embed_more(slot, moved, have):
    columns, count = have.shape
    block = min(512, count)
    return pl.pallas_call(
        more_kernel,
        grid=(count // block,),
        in_specs=[
            pl.BlockSpec((1, block), lambda i: (0, i)),
            pl.BlockSpec(moved.shape, lambda i: (0, 0, 0)),
            pl.BlockSpec((columns, block), lambda i: (0, i)),
        ],
        out_specs=pl.BlockSpec((columns, block), lambda i: (0, i)),
        out_shape=shape((columns, count), BF),
        compiler_params=params(),
        name="embed_more",
    )(slot, moved, have)


def bucket_kernel(slot_ref, data_ref, out_ref):
    slots = out_ref.shape[2]
    count = slot_ref.shape[1]
    start = pl.program_id(0) * slots
    match = hot(rows_like((slots, count)) == slot_ref[...] - start)
    out_ref[0] = dot_nt(data_ref[...], match).astype(BF)


def bucket(slot, data, groups, slots):
    columns, count = data.shape
    return pl.pallas_call(
        bucket_kernel,
        grid=(groups,),
        in_specs=[
            pl.BlockSpec((1, count), lambda i: (0, 0)),
            pl.BlockSpec(data.shape, lambda i: (0, 0)),
        ],
        out_specs=pl.BlockSpec((1, columns, slots), lambda i: (i, 0, 0)),
        out_shape=shape((groups, columns, slots), BF),
        compiler_params=params(),
        cost_estimate=cost(0.2),
        name="bucket",
    )(slot, data)


def know_grad_kernel(where_ref, code_ref, data_ref, out_ref, *, base):
    size = out_ref.shape[2]
    count = code_ref.shape[1]
    step = pl.program_id(0)
    start = (where_ref[0] ^ (base + 4 * (step % 2) + step // 2)) * size
    first = start // KNOW
    last = (start + size - 1) // KNOW
    rows = rows_like((size, count)) + start
    match = rows == code_ref[pl.ds(first, 1), :] + first * KNOW
    match = match | (rows == code_ref[pl.ds(last, 1), :] + last * KNOW)
    out_ref[0] = dot_nt(data_ref[...], hot(match)).astype(BF)


def know_grads(turned, codes, data, base):
    columns = data.shape[0]
    size = TABLES * KNOW // SHARDS
    return pl.pallas_call(
        partial(know_grad_kernel, base=base),
        grid_spec=pltpu.PrefetchScalarGridSpec(
            num_scalar_prefetch=1,
            grid=(4,),
            in_specs=[
                pl.BlockSpec(codes.shape, lambda i, s: (0, 0)),
                pl.BlockSpec(data.shape, lambda i, s: (0, 0)),
            ],
            out_specs=pl.BlockSpec((1, columns, size), lambda i, s: (i, 0, 0)),
        ),
        out_shape=shape((4, columns, size), BF),
        compiler_params=params(),
        cost_estimate=cost(0.2),
        name="know_grads",
    )(turned[None], codes, data)


def collect_kernel(list_ref, sent_ref, out_ref):
    groups, columns, slots = sent_ref.shape
    block = out_ref.shape[1]
    start = pl.program_id(0) * block
    total = jnp.zeros((columns, block), F32)
    for n in range(groups):
        match = hot(lanes_like((slots, block)) == list_ref[n] - start)
        total += dot_nn(sent_ref[n], match)
    out_ref[...] = total


def collect(lists, sent, owned):
    groups, columns, slots = sent.shape
    block = 512
    return pl.pallas_call(
        collect_kernel,
        grid=(pl.cdiv(owned, block),),
        in_specs=[
            pl.BlockSpec(lists.shape, lambda i: (0, 0, 0)),
            pl.BlockSpec(sent.shape, lambda i: (0, 0, 0)),
        ],
        out_specs=pl.BlockSpec((columns, block), lambda i: (0, i)),
        out_shape=shape((columns, owned), F32),
        compiler_params=params(),
        cost_estimate=cost(0.2),
        name="collect",
    )(lists, sent)


def add_know_kernel(where_ref, have_ref, *refs, order, window):
    know_refs, out_ref, table_ref = refs[:-2], refs[-2], refs[-1]
    columns, size = know_refs[0].shape
    step = pl.program_id(0)

    @pl.when(step == 0)
    def _():
        for k, know_ref in enumerate(know_refs):
            table_ref[:, order[k] * size : (order[k] + 1) * size] = know_ref[...]

    block = out_ref.shape[1]
    origin = step * block - where_ref[0]
    base = jnp.clip((origin // 128) * 128, 0, len(know_refs) * size - window)
    base = pl.multiple_of(base, 128)
    shift = rows_like((window, block)) + base == lanes_like((window, block)) + origin
    out_ref[...] = have_ref[...] + dot_nn(table_ref[:, pl.ds(base, window)], hot(shift))


def add_know(offset, have, know, order):
    columns, owned = have.shape
    block = 1024
    part = pl.BlockSpec((columns, block), lambda i, s: (0, i))
    return pl.pallas_call(
        partial(add_know_kernel, order=order, window=block + 128),
        grid_spec=pltpu.PrefetchScalarGridSpec(
            num_scalar_prefetch=1,
            grid=(pl.cdiv(owned, block),),
            in_specs=[part] + [pl.BlockSpec(k.shape, lambda i, s: (0, 0)) for k in know],
            out_specs=part,
            scratch_shapes=[pltpu.VMEM((columns, TABLES * KNOW), BF)],
        ),
        out_shape=shape((columns, owned), F32),
        input_output_aliases={1: 0},
        compiler_params=params(),
        cost_estimate=cost(0.2),
        name="add_know",
    )(offset[None], have, *know)


def collect_more_kernel(list_ref, sent_ref, have_ref, out_ref):
    groups, columns, slots = sent_ref.shape
    block = out_ref.shape[1]
    start = pl.program_id(0) * block
    total = have_ref[...]
    for n in range(groups):
        match = hot(lanes_like((slots, block)) == list_ref[n] - start)
        total += dot_nn(sent_ref[n], match)
    out_ref[...] = total


def collect_more(lists, sent, have):
    columns, owned = have.shape
    block = 512
    return pl.pallas_call(
        collect_more_kernel,
        grid=(pl.cdiv(owned, block),),
        in_specs=[
            pl.BlockSpec(lists.shape, lambda i: (0, 0, 0)),
            pl.BlockSpec(sent.shape, lambda i: (0, 0, 0)),
            pl.BlockSpec((columns, block), lambda i: (0, i)),
        ],
        out_specs=pl.BlockSpec((columns, block), lambda i: (0, i)),
        out_shape=shape((columns, owned), F32),
        compiler_params=params(),
        name="collect_more",
    )(lists, sent, have)


def project_kernel(where_ref, e0, e1, e2, e3, gain_ref, shift_ref, w_ref, bias_ref, f_ref, p_ref):
    pieces = [e[...].astype(F32) for e in (e0, e1, e2, e3)]
    part = pieces[0].shape[0]
    width = 4 * part
    average = sum(jnp.sum(p, 0, keepdims=True) for p in pieces) / width
    pieces = [p - average for p in pieces]
    spread = sum(jnp.sum(p * p, 0, keepdims=True) for p in pieces) / width
    scale = lax.rsqrt(spread + norm_eps)
    for j in range(4):
        rows = pl.ds(pl.multiple_of((where_ref[0] ^ j) * part, 64), part)
        unit = pieces[j] * scale
        f_ref[rows, :] = (unit * gain_ref[rows, :] + shift_ref[rows, :]).astype(BF)
    p_ref[...] = (dot_nn(w_ref[...], f_ref[...]) + bias_ref[...]).astype(BF)


def project(place, pieces, gain, shift, weight, bias):
    part, count = pieces[0].shape
    block = count // 4

    def piece_spec(j):
        return pl.BlockSpec((part, block), lambda i, s: (0, i ^ j))

    return pl.pallas_call(
        project_kernel,
        grid_spec=pltpu.PrefetchScalarGridSpec(
            num_scalar_prefetch=1,
            grid=(4,),
            in_specs=[piece_spec(j) for j in range(4)]
            + [whole(gain.shape), whole(shift.shape), whole(weight.shape), whole(bias.shape)],
            out_specs=[
                pl.BlockSpec((4 * part, block), lambda i, s: (0, i)),
                pl.BlockSpec((weight.shape[0], block), lambda i, s: (0, i)),
            ],
        ),
        out_shape=[shape((4 * part, count), BF), shape((weight.shape[0], count), BF)],
        compiler_params=params(),
        cost_estimate=cost(8),
        name="project",
    )(place[None], *pieces, gain, shift, weight, bias)


def two_parts(value):
    high = value.astype(BF).astype(F32)
    return high, value - high


def widened(part, head, head_dim, extra):
    columns, count = part.shape
    rows = rows_like((columns, count))
    keep = (rows >= head * head_dim) & (rows < (head + 1) * head_dim)
    kept = jnp.where(keep, part, 0.0)
    below = rows_like((256 - columns, count))
    rest = jnp.zeros((256 - columns, count), F32)
    for at, row in enumerate(extra):
        rest = jnp.where(below == at, row, rest)
    return jnp.concatenate([kept, rest], 0).astype(BF)


def attend_kernel(q_ref, kv_ref, mask_ref, out_ref, lse_ref, keys_ref, *, heads, head_dim):
    columns = heads * head_dim
    count = kv_ref.shape[1]

    @pl.when(pl.program_id(0) == 0)
    def _():
        rest = rows_like((256 - columns, count))
        rest = jnp.where(rest == 0, mask_ref[...], 0.0)
        k = kv_ref[columns : 2 * columns, :].astype(F32)
        keys_ref[...] = jnp.concatenate([k, rest], 0).T.astype(BF)

    queries = q_ref[...].astype(F32) * head_dim ** (-0.5)
    ones = jnp.ones((1, queries.shape[1]), F32)
    for h in range(heads):
        scores = dot_nn(keys_ref[...], widened(queries, h, head_dim, [ones]))
        highest = jnp.max(scores, 0, keepdims=True)
        expanded = jnp.exp(scores - highest)
        total = jnp.sum(expanded, 0, keepdims=True)
        rows = slice(h * head_dim, (h + 1) * head_dim)
        values = kv_ref[2 * columns + h * head_dim : 2 * columns + (h + 1) * head_dim, :]
        out_ref[rows, :] = (dot_nn(values, expanded.astype(BF)) / total).astype(BF)
        lse_ref[h : h + 1, :] = highest + jnp.log(total)


def attend(qkv, mask, half, heads, head_dim):
    count = qkv.shape[1]
    columns = heads * head_dim
    block = 256
    steps = count // block // 2
    return pl.pallas_call(
        partial(attend_kernel, heads=heads, head_dim=head_dim),
        grid=(steps,),
        in_specs=[
            pl.BlockSpec((columns, block), lambda i: (0, steps * half + i)),
            pl.BlockSpec(qkv.shape, lambda i: (0, 0)),
            pl.BlockSpec((1, count), lambda i: (0, 0)),
        ],
        out_specs=[
            pl.BlockSpec((columns, block), lambda i: (0, i)),
            pl.BlockSpec((8, block), lambda i: (0, i)),
        ],
        out_shape=[shape((columns, count // 2), BF), shape((8, count // 2), F32)],
        scratch_shapes=[pltpu.VMEM((count, 256), BF)],
        compiler_params=params(),
        cost_estimate=cost(16),
        name="attend",
    )(qkv, qkv, mask)


def attend_back_kernel(
    q_ref, kv_ref, mask_ref, o_ref, g_ref, lse_ref, d_ref,
    keys_ref, values_ref, dk_acc, dv_acc, *, heads, head_dim,
):
    step = pl.program_id(0)
    columns = heads * head_dim
    count = kv_ref.shape[1]
    block = q_ref.shape[1]

    @pl.when(step == 0)
    def _():
        rest = rows_like((256 - columns, count))
        ones = jnp.where((rest == 1) | (rest == 2), 1.0, 0.0)
        with_mask = jnp.where(rest == 0, mask_ref[...], ones)
        k = kv_ref[columns : 2 * columns, :].astype(F32)
        v = kv_ref[2 * columns : 3 * columns, :].astype(F32)
        keys_ref[...] = jnp.concatenate([k, with_mask], 0).T.astype(BF)
        values_ref[...] = jnp.concatenate([v, ones], 0).T.astype(BF)
        dk_acc[...] = jnp.zeros_like(dk_acc)
        dv_acc[...] = jnp.zeros_like(dv_acc)

    score_scale = head_dim ** (-0.5)
    queries = q_ref[...].astype(F32) * score_scale
    grads = g_ref[...].astype(F32)
    inner = grads * o_ref[...].astype(F32)
    by_query = queries.T
    by_grad = grads.T
    lanes = lanes_like(by_query.shape)
    one = jnp.ones((1, block), F32)
    zero = jnp.zeros((1, block), F32)
    here = pl.ds(pl.multiple_of(step * block, 128), block)
    for h in range(heads):
        rows = slice(h * head_dim, (h + 1) * head_dim)
        keep = (lanes >= h * head_dim) & (lanes < (h + 1) * head_dim)
        lse = two_parts(-lse_ref[h : h + 1, :])
        delta = two_parts(-jnp.sum(inner[rows, :], 0, keepdims=True))
        scores = dot_nn(keys_ref[...], widened(queries, h, head_dim, [one, *lse]))
        probs = jnp.exp(scores)
        dv_acc[...] += dot_nn(probs.astype(BF), jnp.where(keep, by_grad, 0.0).astype(BF))
        grad_probs = dot_nn(values_ref[...], widened(grads, h, head_dim, [zero, *delta]))
        grad_scores = (probs * grad_probs).astype(BF)
        dk_acc[...] += dot_nn(grad_scores, jnp.where(keep, by_query, 0.0).astype(BF))
        keys = kv_ref[columns + h * head_dim : columns + (h + 1) * head_dim, :]
        d_ref[rows, here] = (dot_nn(keys, grad_scores) * score_scale).astype(BF)

    @pl.when(step == pl.num_programs(0) - 1)
    def _():
        d_ref[columns : 2 * columns, :] = dk_acc[...].T.astype(BF)
        d_ref[2 * columns :, :] = dv_acc[...].T.astype(BF)


def attend_back(qkv, mask, out, grad, lse, heads, head_dim):
    count = qkv.shape[1]
    columns = heads * head_dim
    block = 256
    part = pl.BlockSpec((columns, block), lambda i: (0, i))
    return pl.pallas_call(
        partial(attend_back_kernel, heads=heads, head_dim=head_dim),
        grid=(count // block,),
        in_specs=[
            part,
            pl.BlockSpec(qkv.shape, lambda i: (0, 0)),
            pl.BlockSpec((1, count), lambda i: (0, 0)),
            part,
            part,
            pl.BlockSpec((8, block), lambda i: (0, i)),
        ],
        out_specs=pl.BlockSpec(qkv.shape, lambda i: (0, 0)),
        out_shape=shape(qkv.shape, BF),
        scratch_shapes=[
            pltpu.VMEM((count, 256), BF),
            pltpu.VMEM((count, 256), BF),
            pltpu.VMEM((count, columns), F32),
            pltpu.VMEM((count, columns), F32),
        ],
        compiler_params=params(),
        cost_estimate=cost(38),
        name="attend_back",
    )(qkv, qkv, mask, out, grad, lse)


def to_second_kernel(where_ref, *refs):
    h_refs, e_refs, o_refs = refs[0:4], refs[4:8], refs[8:12]
    vec_ref, resid_ref, second_ref, emb_ref = refs[12:]
    part = h_refs[0].shape[0]
    for j in range(4):
        rows = pl.ds(pl.multiple_of((where_ref[0] ^ j) * part, 64), part)
        emb_ref[rows, :] = e_refs[j][...].astype(F32)
    resid = emb_ref[...].T + vec_ref[0:1, :]
    for j in range(4):
        resid += dot_tn(h_refs[j][...], o_refs[j][...])
    resid_ref[...] = resid
    centered = resid - jnp.mean(resid, -1, keepdims=True)
    spread = jnp.mean(centered * centered, -1, keepdims=True)
    unit = centered * lax.rsqrt(spread + norm_eps)
    second_ref[...] = (unit * vec_ref[1:2, :] + vec_ref[2:3, :]).astype(BF)


def to_second(place, heads, pieces, outs, vectors):
    part, count = heads[0].shape
    width = outs[0].shape[1]
    block = 256
    steps = count // block

    def piece_spec(j):
        return pl.BlockSpec((part, block), lambda i, s: (0, steps * j + i))

    lane = pl.BlockSpec((part, block), lambda i, s: (0, i))
    token = pl.BlockSpec((block, width), lambda i, s: (i, 0))
    return pl.pallas_call(
        to_second_kernel,
        grid_spec=pltpu.PrefetchScalarGridSpec(
            num_scalar_prefetch=1,
            grid=(steps,),
            in_specs=[lane] * 4
            + [piece_spec(j) for j in range(4)]
            + [whole(w.shape) for w in outs]
            + [whole(vectors.shape)],
            out_specs=[token, token],
            scratch_shapes=[pltpu.VMEM((width, block), F32)],
        ),
        out_shape=[shape((count, width), F32), shape((count, width), BF)],
        compiler_params=params(),
        cost_estimate=cost(4),
        name="to_second",
    )(place[None], *heads, *pieces, *outs, vectors)


def feed_kernel(second_ref, g_ref, up_ref, down_ref, bias_ref, act_ref, pre_ref, grad_ref):
    pre_act = dot_nn(second_ref[...], up_ref[...]) + bias_ref[...]
    inside = 0.5 * (1.0 + lax.erf(pre_act * (0.5**0.5)))
    density = jnp.exp(-0.5 * pre_act * pre_act) * 0.3989422804014327
    act_ref[...] = (pre_act * inside).astype(BF)
    grad_act = dot_nt(g_ref[...], down_ref[...])
    grad_pre = (grad_act * (inside + pre_act * density)).astype(BF)
    pre_ref[...] = grad_pre
    grad_ref[...] = dot_nt(grad_pre, up_ref[...]).astype(BF)


def feed_block(second, grad_out, up, down, bias):
    count, width = second.shape
    units = up.shape[1]
    block = 256
    token = pl.BlockSpec((block, width), lambda i: (i, 0))
    unit = pl.BlockSpec((block, units), lambda i: (i, 0))
    return pl.pallas_call(
        feed_kernel,
        grid=(count // block,),
        in_specs=[token, token, whole(up.shape), whole(down.shape), whole(bias.shape)],
        out_specs=[unit, unit, token],
        out_shape=[
            shape((count, units), BF),
            shape((count, units), BF),
            shape((count, width), BF),
        ],
        compiler_params=params(),
        cost_estimate=cost(4),
        name="feed_block",
    )(second, grad_out, up, down, bias)


def feed_weight_kernel(*refs):
    s_refs, p_refs, a_refs, g_refs = refs[0:4], refs[4:8], refs[8:12], refs[12:16]
    out_ref, sum_ref = refs[16:]
    up = sum(dot_tn(s_refs[j][...], p_refs[j][...]) for j in range(4))
    out_ref[0] = up.astype(BF)
    down = sum(dot_tn(a_refs[j][...], g_refs[j][...]) for j in range(4))
    out_ref[1] = down.astype(BF)
    total = sum(jnp.sum(p[...].astype(F32), 0, keepdims=True) for p in p_refs)
    sum_ref[...] = jnp.broadcast_to(total, sum_ref.shape)


def feed_weights(seconds, grad_pres, activated, grad_outs):
    width, units = seconds[0].shape[1], grad_pres[0].shape[1]
    arrays = (*seconds, *grad_pres, *activated, *grad_outs)
    return pl.pallas_call(
        feed_weight_kernel,
        grid=(1,),
        in_specs=[whole(a.shape) for a in arrays],
        out_specs=[whole((2, width, units)), whole((8, units))],
        out_shape=[shape((2, width, units), BF), shape((8, units), F32)],
        compiler_params=params(),
        cost_estimate=cost(9),
        name="feed_weights",
    )(*arrays)


def to_heads_kernel(resid_ref, a_ref, b_ref, c_ref, g_ref, *refs):
    o_refs = refs[0:4]
    vec_ref, low_ref, grad_ref, heads_ref, sums_ref = refs[4:]
    resid = resid_ref[...]
    centered = resid - jnp.mean(resid, -1, keepdims=True)
    spread = jnp.mean(centered * centered, -1, keepdims=True)
    scale = lax.rsqrt(spread + norm_eps)
    unit = centered * scale
    grad_second = a_ref[...].astype(F32) + b_ref[...].astype(F32) + c_ref[...].astype(F32)
    e = grad_second * vec_ref[1:2, :]
    first_mean = jnp.mean(e, -1, keepdims=True)
    second_mean = jnp.mean(e * unit, -1, keepdims=True)
    grad_out = g_ref[...].astype(F32)
    grad_resid = grad_out + scale * (e - first_mean - unit * second_mean)
    low = grad_resid.astype(BF)
    low_ref[...] = low
    grad_ref[...] = grad_resid.T
    for j in range(4):
        heads_ref[j] = dot_nt(o_refs[j][...], low).astype(BF)
    rows = [grad_second * unit, grad_second, grad_resid, grad_out]
    rows = [jnp.sum(r, 0, keepdims=True) for r in rows]
    blank = jnp.zeros_like(rows[0])

    @pl.when(pl.program_id(0) == 0)
    def _():
        sums_ref[...] = jnp.zeros_like(sums_ref)

    sums_ref[...] += jnp.concatenate(rows + [blank] * 4, 0)


def to_heads(resid, terms, grad_out, outs, vectors):
    count, width = resid.shape
    part = outs[0].shape[0]
    block = 256
    token = pl.BlockSpec((block, width), lambda i: (i, 0))
    return pl.pallas_call(
        to_heads_kernel,
        grid=(count // block,),
        in_specs=[token] * 5 + [whole(w.shape) for w in outs] + [whole(vectors.shape)],
        out_specs=[
            token,
            pl.BlockSpec((width, block), lambda i: (0, i)),
            pl.BlockSpec((4, part, block), lambda i: (0, 0, i)),
            whole((8, width)),
        ],
        out_shape=[
            shape((count, width), BF),
            shape((width, count), F32),
            shape((4, part, count), BF),
            shape((8, width), F32),
        ],
        compiler_params=params(),
        cost_estimate=cost(5),
        name="to_heads",
    )(resid, *terms, grad_out, *outs, vectors)


def rest_kernel(near_ref, far_ref, l0, l1, l2, l3, back_ref, first_ref, out_ref):
    columns, half = near_ref.shape
    quarter = half // 2
    total = dot_nn(near_ref[:, :quarter], l0[...]) + dot_nn(near_ref[:, quarter:], l1[...])
    total += dot_nn(far_ref[:, :quarter], l2[...]) + dot_nn(far_ref[:, quarter:], l3[...])
    out_ref[:columns, :] = total.astype(BF)
    out_ref[columns:, :] = dot_nt(back_ref[...], first_ref[...]).astype(BF)


def rest_weights(near, far, lows, back, first):
    width = first.shape[0]
    arrays = (near, far, *lows, back, first)
    dims = (near.shape[0] + back.shape[0], width)
    return pl.pallas_call(
        rest_kernel,
        grid=(1,),
        in_specs=[whole(a.shape) for a in arrays],
        out_specs=whole(dims),
        out_shape=shape(dims, BF),
        compiler_params=params(),
        cost_estimate=cost(6),
        name="rest_weights",
    )(*arrays)


def finish_kernel(
    where_ref, a_ref, b_ref, c_ref, e0, e1, e2, e3, resid_ref, gain_ref,
    cols_ref, rows_ref, sums_ref, emb_ref,
):
    part = e0.shape[0]
    width = 4 * part
    for j, e in enumerate((e0, e1, e2, e3)):
        rows = pl.ds(pl.multiple_of((where_ref[0] ^ j) * part, 64), part)
        emb_ref[rows, :] = e[...].astype(F32)
    grad = a_ref[...].astype(F32) + b_ref[...].astype(F32) + c_ref[...].astype(F32)
    values = emb_ref[...]
    centered = values - jnp.sum(values, 0, keepdims=True) / width
    spread = jnp.sum(centered * centered, 0, keepdims=True) / width
    scale = lax.rsqrt(spread + norm_eps)
    unit = centered * scale
    e = grad * gain_ref[...]
    first_mean = jnp.sum(e, 0, keepdims=True) / width
    second_mean = jnp.sum(e * unit, 0, keepdims=True) / width
    total = resid_ref[...] + scale * (e - first_mean - unit * second_mean)
    emb_ref[...] = total
    for j in range(4):
        rows = pl.ds(pl.multiple_of((where_ref[0] ^ j) * part, 64), part)
        cols_ref[j] = emb_ref[rows, :].astype(BF)
    rows_ref[...] = total.T.astype(BF)
    sums_ref[:, 0:1] = jnp.sum(grad * unit, 1, keepdims=True)
    sums_ref[:, 1:2] = jnp.sum(grad, 1, keepdims=True)


def finish(place, a, b, c, pieces, resid, gain):
    width, count = a.shape
    part = pieces[0].shape[0]

    def piece_spec(j):
        return pl.BlockSpec((part, count), lambda i, s: (0, j))

    return pl.pallas_call(
        finish_kernel,
        grid_spec=pltpu.PrefetchScalarGridSpec(
            num_scalar_prefetch=1,
            grid=(1,),
            in_specs=[whole(a.shape)] * 3
            + [piece_spec(j) for j in range(4)]
            + [whole(resid.shape), whole(gain.shape)],
            out_specs=[whole((4, part, count)), whole((count, width)), whole((width, 128))],
            scratch_shapes=[pltpu.VMEM((width, count), F32)],
        ),
        out_shape=[
            shape((4, part, count), BF),
            shape((count, width), BF),
            shape((width, 128), F32),
        ],
        compiler_params=params(),
        cost_estimate=cost(4),
        name="finish",
    )(place[None], a, b, c, *pieces, resid, gain)


def body(
    gene_ids,
    know_ids,
    lengths,
    tables,
    norm_gain,
    norm_bias,
    qkv_weight,
    qv_bias,
    out_weight,
    out_bias,
    up_weight,
    up_bias,
    down_weight,
    down_bias,
    cotangent,
):
    count = gene_ids.shape[0]
    width = norm_gain.shape[1]
    columns = qkv_weight.shape[2]
    units = up_weight.shape[1]
    head_dim = width // HEADS
    heads_here = columns // head_dim
    owned = tables.shape[0]
    groups = lax.axis_size("dp")
    place = lax.axis_index("tensor")
    group = lax.axis_index("dp")
    quarter = count // 4
    length = lengths[0]
    slots = 128 * (-(-(3 * count // (2 * groups)) // 128))
    know_rows = TABLES * KNOW
    share = know_rows // SHARDS
    start = VOCAB - (groups - 1) * owned
    one_owner = start >= 0 and groups == SHARDS

    def block_at(value, j, size, axis=0):
        return lax.dynamic_slice_in_dim(value, (place ^ j) * size, size, axis)

    def relative(value, size, axis=0):
        return jnp.concatenate([block_at(value, j, size, axis) for j in range(4)], axis)

    ids = relative(gene_ids, quarter)[None]
    codes = relative(know_ids, quarter, 1)
    step = 1
    while step < groups:
        ids = jnp.concatenate([ids, hop(ids, "dp", step)], 0)
        step *= 2
    lists, slot, most = route(group, jnp.int32(0), ids, owned, slots)
    rounds = (most[0, 0] + slots - 1) // slots

    table = tables.T

    if one_owner:
        held = table[:, start : start + know_rows]
        shards = [held[:, i * share : (i + 1) * share] for i in range(SHARDS)]
        dealt = [lax.ppermute(shards[i], "dp", [(groups - 1, i)]) for i in range(groups - 1)]
        mine = jnp.where(group == groups - 1, shards[-1], jnp.zeros((), BF))
        mine = sum(after(dealt, lists), mine)
        lists = after(lists, mine)
        know = lax.all_gather(mine, "dp")
        turned = group
    else:
        room = jnp.pad(table, ((0, 0), (know_rows, know_rows)))
        begin = jnp.clip(VOCAB - group * owned + know_rows, 0, owned + know_rows)
        know = lax.psum(lax.dynamic_slice_in_dim(room, begin, know_rows, 1), "dp")
        know = jnp.stack([know[:, i * share : (i + 1) * share] for i in range(SHARDS)])
        turned = jnp.int32(0)

    def exchange(blocks):
        return lax.all_to_all(blocks, "dp", 0, 0, tiled=True)

    out_blocks = gather_four(out_weight)
    moved = exchange(pick(lists, table))
    moved = after(moved, *out_blocks)
    summed = embed(slot, codes, moved, know)

    def more_rows(carry):
        turn, total = carry
        these, at, _ = route(group, turn, ids, owned, slots)
        return turn + 1, embed_more(at, exchange(pick(these, table)), total)

    _, summed = lax.while_loop(lambda c: c[0] < rounds, more_rows, (jnp.int32(1), summed))
    pieces = gather_four(summed)

    gain = norm_gain.astype(F32)
    shift = norm_bias.astype(F32)
    weight = qkv_weight.transpose(0, 2, 1).reshape(3 * columns, width)
    bias = qv_bias.astype(F32)
    bias = jnp.concatenate([bias[0], jnp.zeros((columns,), F32), bias[1]])[:, None]
    first, qkv = project(place, pieces, gain[0][:, None], shift[0][:, None], weight, bias)
    spots = relative(jnp.arange(count, dtype=I32), quarter)
    mask = jnp.where(spots < length, 0.0, -1e30).astype(F32)[None]
    far_heads, far_lse = attend(qkv, mask, 1, heads_here, head_dim)
    near_heads, near_lse = attend(qkv, after(mask, far_heads), 0, heads_here, head_dim)
    heads_out = jnp.concatenate([near_heads, far_heads], 1)
    lse = jnp.concatenate([near_lse, far_lse], 1)

    heads = [near_heads, far_heads]
    heads = swap_four([heads[j // 2][:, (j % 2) * quarter :][:, :quarter] for j in range(4)])
    valid = jnp.arange(count, dtype=I32) < length
    grad_full = cotangent * valid[:, None].astype(BF)
    grad_outs = [block_at(grad_full, j, quarter) for j in range(4)]
    grad_out = grad_outs[0]
    vectors = jnp.stack([out_bias.astype(F32), gain[1], shift[1]])
    resid, second = to_second(place, heads, pieces, out_blocks, vectors)
    up_row = up_bias.astype(F32)[None]

    def feed(j, rows):
        return feed_block(rows, grad_outs[j], up_weight, down_weight, up_row)

    far = hop(second, "tensor", 2)
    seconds = [second, hop(second, "tensor", 1)]
    blocks = [feed(0, seconds[0]), feed(1, seconds[1])]
    far = after(far, blocks)
    seconds += [far, hop(far, "tensor", 1)]
    blocks += [feed(2, seconds[2]), feed(3, seconds[3])]
    activated, grad_pres, grad_seconds = zip(*blocks)
    two = grad_seconds[2].astype(F32) + hop(grad_seconds[3], "tensor", 1).astype(F32)
    from_far = hop(two.astype(BF), "tensor", 2)
    from_near = hop(grad_seconds[1], "tensor", 1)
    feed_part, unit_sums = feed_weights(
        seconds, grad_pres, activated, [after(g, two) for g in grad_outs]
    )
    low, grad_resid, grad_heads, sums = to_heads(
        resid,
        after((grad_seconds[0], from_near, from_far), feed_part),
        grad_out,
        out_blocks,
        vectors,
    )
    grads = jnp.concatenate(swap_four([grad_heads[j] for j in range(4)]), 1)

    lows = swap_four([low] * 4)
    back = attend_back(qkv, mask, heads_out, grads, lse, heads_here, head_dim)

    def sum_four(parts):
        two = parts[2].astype(F32) + hop(parts[3], "tensor", 1).astype(F32)
        zero = parts[0].astype(F32) + hop(parts[1], "tensor", 1).astype(F32)
        return zero + hop(two.astype(BF), "tensor", 2).astype(F32)

    feed_grad = lax.psum(feed_part, "dp")

    def first_grad(j):
        return dot_tn(weight, back[:, j * quarter : (j + 1) * quarter]).astype(BF)

    two = first_grad(2).astype(F32) + hop(first_grad(3), "tensor", 1).astype(F32)
    later, back_later = after((activated, back), two)
    rest = rest_weights(near_heads, far_heads, lows, back_later, first)
    feeds = [dot_nn(after(later[j], rest), down_weight).astype(BF) for j in range(4)]
    from_far = hop(two.astype(BF), "tensor", 2)
    from_near = hop(first_grad(1), "tensor", 1)
    by_column, by_row, first_sums = finish(
        place, first_grad(0), from_near, from_far, pieces, grad_resid, gain[0][:, None]
    )
    grad_columns = jnp.concatenate(swap_four([by_column[j] for j in range(4)]), 1)

    odd_part = know_grads(turned, codes, grad_columns, 2)
    even_part = know_grads(turned, after(codes, odd_part), grad_columns, 0)
    dealt = bucket(after(slot, even_part), grad_columns, groups, slots)
    sent = exchange(dealt)
    downs = after(lists, qkv).transpose(0, 2, 1)
    tables_grad = collect(downs, sent, owned)
    if one_owner:

        def pair_sum(part):
            own = part[:2].astype(F32)
            return own + hop(part[2:], "dp", 1).astype(F32)

        odd_sum = hop(pair_sum(odd_part).astype(BF), "dp", 2)
        even_sum = pair_sum(even_part) + odd_sum.astype(F32)
        know_sum = even_sum[0] + hop(even_sum[1].astype(BF), "dp", 4).astype(F32)
        know_sum = know_sum.astype(BF)
        last = jnp.where(group == groups - 1, know_sum, jnp.zeros((), BF))
        know_all = [lax.ppermute(know_sum, "dp", [(i, groups - 1)]) for i in range(groups - 1)]
        know_all, order = know_all + [last], tuple(range(SHARDS))
    else:
        know_all = lax.psum(jnp.concatenate([even_part, odd_part], 0), "dp")
        know_all, order = [know_all[k] for k in range(SHARDS)], (0, 4, 1, 5, 2, 6, 3, 7)

    def more_grads(carry):
        turn, total = carry
        these, at, _ = route(group, turn, ids, owned, slots)
        these = these.transpose(0, 2, 1)
        return turn + 1, collect_more(these, exchange(bucket(at, grad_columns, groups, slots)), total)

    _, tables_grad = lax.while_loop(
        lambda c: c[0] < rounds, more_grads, (jnp.int32(1), tables_grad)
    )

    feeds = after(feeds, grad_columns)
    out_own = (resid + sum_four(feeds) + down_bias.astype(F32)).astype(BF)

    def spread_rows(own, kind):
        full = jnp.zeros((count, width), kind)
        for j, block in enumerate(gather_four(own)):
            full = lax.dynamic_update_slice_in_dim(
                full, block.astype(kind), (place ^ j) * quarter, 0
            )
        return full

    out = spread_rows(after(out_own, grad_columns), BF)
    input_grad = spread_rows(after(by_row, grad_columns), F32)

    rest = lax.psum(after(rest, feed_grad), "dp")
    feed_grad = after(feed_grad, sent).astype(F32)

    qv = jnp.sum(back.reshape(3, columns, count).astype(F32), -1)
    qv = jnp.stack([qv[0], qv[2]])
    qv_wide = lax.dynamic_update_slice_in_dim(
        jnp.zeros((2, width), F32), qv, place * columns, 1
    )
    up_sums = lax.dynamic_update_slice_in_dim(
        jnp.zeros((4, units), F32), unit_sums[0:1], place, 0
    )
    packed = jnp.concatenate(
        [
            first_sums[:, 0],
            first_sums[:, 1],
            sums[0:4].reshape(-1),
            qv_wide.reshape(-1),
            up_sums.reshape(-1),
        ]
    ).reshape(-1, 128)
    packed = after(packed, sent)
    for step in (1, 2):
        packed = packed + hop(packed, "tensor", step)
    step = 1
    while step < groups:
        packed = packed + hop(packed, "dp", step)
        step *= 2
    packed = packed.reshape(-1)
    know_all = after(know_all, packed, out, input_grad, feed_grad)
    tables_grad = add_know(VOCAB - group * owned, tables_grad, know_all, order)
    rest = after(rest, tables_grad).astype(F32)
    outw_grad = rest[:columns]
    qkv_grad = rest[columns:].reshape(3, columns, width).transpose(0, 2, 1)
    tops = packed[: 6 * width].reshape(6, width)
    qv_wide = packed[6 * width : 8 * width].reshape(2, width)
    up_sums = packed[8 * width :].reshape(4, units)
    return (
        out,
        input_grad,
        tables_grad.T,
        jnp.stack([tops[0], tops[2]]),
        jnp.stack([tops[1], tops[3]]),
        qkv_grad,
        lax.dynamic_slice_in_dim(qv_wide, place * columns, columns, 1),
        outw_grad,
        tops[4],
        feed_grad[0],
        lax.dynamic_slice_in_dim(up_sums, place, 1, 0)[0],
        feed_grad[1],
        tops[5],
    )


def solution(mesh):
    placed = (
        P("dp"),
        P(None, "dp"),
        P("dp"),
        P("dp", "tensor"),
        P(),
        P(),
        P(None, None, "tensor"),
        P(None, "tensor"),
        P("tensor", None),
        P(),
        P(None, "tensor"),
        P("tensor"),
        P("tensor", None),
        P(),
        P("dp", None),
    )
    return jax.shard_map(
        body,
        mesh=mesh,
        in_specs=placed,
        out_specs=(
            P("dp", None),
            P("dp", None),
            P("dp", "tensor"),
            P(),
            P(),
            P(None, None, "tensor"),
            P(None, "tensor"),
            P("tensor", None),
            P(),
            P(None, "tensor"),
            P("tensor"),
            P("tensor", None),
            P(),
        ),
        check_vma=False,
    )
```

```python
from functools import partial

import jax
import jax.numpy as jnp
from jax import lax
from jax.experimental import pallas as pl
from jax.experimental.pallas import tpu as pltpu
from jax.sharding import PartitionSpec as P

HEADS = 12
VOCAB = 36000
KNOW = 1024
TABLES = 5
SHARDS = 8
norm_eps = 1e-05
BF = jnp.bfloat16
F32 = jnp.float32
I32 = jnp.int32
BIG = 56 * 1024 * 1024


def params():
    return pltpu.CompilerParams(vmem_limit_bytes=BIG)


def cost(micros):
    return pl.CostEstimate(
        flops=int(micros * 9e8), bytes_accessed=int(micros * 3e6), transcendentals=0
    )


def shape(dims, kind):
    return jax.ShapeDtypeStruct(dims, kind)


def dot_nt(left, right):
    return lax.dot_general(left, right, (((1,), (1,)), ((), ())), preferred_element_type=F32)


def dot_tn(left, right):
    return lax.dot_general(left, right, (((0,), (0,)), ((), ())), preferred_element_type=F32)


def dot_nn(left, right):
    return jnp.dot(left, right, preferred_element_type=F32)


def whole(dims):
    return pl.BlockSpec(dims, lambda i, *s: (0,) * len(dims))


def hot(condition):
    return condition.astype(F32).astype(BF)


def rows_like(dims):
    return lax.broadcasted_iota(I32, dims, 0)


def lanes_like(dims):
    return lax.broadcasted_iota(I32, dims, 1)


def after(value, *others):
    return lax.optimization_barrier((value, others))[0]


def hop(value, axis, flip):
    count = lax.axis_size(axis)
    return lax.ppermute(value, axis, [(i, i ^ flip) for i in range(count)])


def gather_four(block):
    far = hop(block, "tensor", 2)
    return [block, hop(block, "tensor", 1), far, hop(far, "tensor", 1)]


def swap_four(pieces):
    return [pieces[0]] + [hop(pieces[j], "tensor", j) for j in (1, 2, 3)]


def route_kernel(where_ref, ids_ref, lists_ref, slot_ref, most_ref, *, owned, slots):
    group, turn = where_ref[0], where_ref[1]
    ids = ids_ref[...]
    groups, count = ids.shape
    wanted = (ids >= group * owned) & (ids < (group + 1) * owned)
    mine = jnp.broadcast_to(ids[0:1, :], (groups, count))
    owners = rows_like((groups, count))
    held = (mine >= owners * owned) & (mine < (owners + 1) * owned)
    flags = jnp.concatenate([wanted.astype(F32), held.astype(F32)], 0)
    sums = flags
    lanes = lanes_like(flags.shape)
    step = 1
    while step < count:
        sums = sums + jnp.where(lanes >= step, pltpu.roll(sums, step, 1), 0.0)
        step *= 2
    low = (turn * slots).astype(F32)
    ranks = sums[:groups] - 1.0 - low
    ranks = jnp.where(wanted & (ranks >= 0.0) & (ranks < slots), ranks, -1.0).astype(I32)
    plus = jnp.where(wanted, ids - group * owned + 1, 0)
    spots = rows_like((slots, count))
    halves = rows_like((16, count))
    for k in range(groups):
        number = jnp.broadcast_to(plus[k : k + 1, :], (16, count))
        parts = jnp.where(halves == 0, number >> 8, jnp.where(halves == 1, number & 255, 0))
        parts = parts.astype(F32).astype(BF)
        match = hot(spots == ranks[k : k + 1, :])
        found = dot_nt(parts, match)
        lists_ref[group ^ k] = (found[0:1, :] * 256.0 + found[1:2, :]).astype(I32) - 1
    own = sums[groups:] - 1.0 - low
    good = held & (own >= 0.0) & (own < slots)
    slot = jnp.where(good, owners.astype(F32) * slots + own + 1.0, 0.0)
    slot = jnp.sum(slot, 0, keepdims=True) - 1.0
    slot_ref[...] = slot.astype(I32)
    most = jnp.zeros((groups, 1), F32)
    for o in range(groups):
        here = (ids >= o * owned) & (ids < (o + 1) * owned)
        most = jnp.maximum(most, jnp.sum(here.astype(F32), 1, keepdims=True))
    most_ref[...] = jnp.broadcast_to(jnp.max(most, 0, keepdims=True), (8, 128)).astype(I32)


def route(group, turn, ids, owned, slots):
    groups, count = ids.shape

    return pl.pallas_call(
        partial(route_kernel, owned=owned, slots=slots),
        grid_spec=pltpu.PrefetchScalarGridSpec(
            num_scalar_prefetch=1,
            grid=(1,),
            in_specs=[whole(ids.shape)],
            out_specs=[
                whole((groups, 1, slots)),
                whole((1, count)),
                whole((8, 128)),
            ],
        ),
        out_shape=[
            shape((groups, 1, slots), I32),
            shape((1, count), I32),
            shape((8, 128), I32),
        ],
        compiler_params=params(),
        cost_estimate=cost(8),
        name="route",
    )(jnp.stack([group, turn]), ids)


def pick_kernel(list_ref, table_ref, out_ref, *, chunk):
    wanted = list_ref[0]
    size = table_ref.shape[1]
    total = jnp.zeros(out_ref.shape[1:], F32)
    for start in range(0, size, chunk):
        part = min(chunk, size - start)
        match = hot(rows_like((part, wanted.shape[1])) == wanted - start)
        total += dot_nn(table_ref[:, start : start + part], match)
    out_ref[0] = total.astype(BF)


def pick(lists, table):
    groups, _, slots = lists.shape
    columns = table.shape[0]
    return pl.pallas_call(
        partial(pick_kernel, chunk=512),
        grid=(groups,),
        in_specs=[
            pl.BlockSpec((1, 1, slots), lambda i: (i, 0, 0)),
            pl.BlockSpec(table.shape, lambda i: (0, 0)),
        ],
        out_specs=pl.BlockSpec((1, columns, slots), lambda i: (i, 0, 0)),
        out_shape=shape((groups, columns, slots), BF),
        compiler_params=params(),
        cost_estimate=cost(12),
        name="pick",
    )(lists, table)


def embed_kernel(
    where_ref, slot_ref, code_ref, moved_ref, know_ref, extra_ref, out_ref, table_ref, *, order
):
    groups, columns, slots = moved_ref.shape
    shards, _, size = know_ref.shape

    @pl.when(pl.program_id(0) == 0)
    def _():
        for k in range(shards):
            at = pl.multiple_of((where_ref[0] ^ order[k]) * size, 128)
            table_ref[:, pl.ds(at, size)] = know_ref[k]

    slot = slot_ref[...]
    block = slot.shape[1]
    total = extra_ref[...].astype(F32)
    for n in range(groups):
        match = hot(rows_like((slots, block)) == slot - n * slots)
        total += dot_nn(moved_ref[n], match)
    for j in range(TABLES):
        match = hot(rows_like((KNOW, block)) == code_ref[j : j + 1, :])
        total += dot_nn(table_ref[:, j * KNOW : (j + 1) * KNOW], match)
    out_ref[...] = total.astype(BF)


def embed(half, turned, order, slot, codes, moved, know, extra):
    count = slot.shape[1] // 2
    columns = moved.shape[1]
    block = min(512, count)
    steps = count // block
    return pl.pallas_call(
        partial(embed_kernel, order=order),
        grid_spec=pltpu.PrefetchScalarGridSpec(
            num_scalar_prefetch=1,
            grid=(steps,),
            in_specs=[
                pl.BlockSpec((1, block), lambda i, s: (0, steps * half + i)),
                pl.BlockSpec((TABLES, block), lambda i, s: (0, steps * half + i)),
                whole(moved.shape),
                whole(know.shape),
                pl.BlockSpec((columns, block), lambda i, s: (0, steps * half + i)),
            ],
            out_specs=pl.BlockSpec((columns, block), lambda i, s: (0, i)),
            scratch_shapes=[pltpu.VMEM((columns, TABLES * KNOW), BF)],
        ),
        out_shape=shape((columns, count), BF),
        compiler_params=params(),
        cost_estimate=cost(6),
        name="embed",
    )(turned[None], slot, codes, moved, know, extra)


def more_kernel(slot_ref, moved_ref, have_ref, out_ref):
    groups, columns, slots = moved_ref.shape
    slot = slot_ref[...]
    block = slot.shape[1]
    total = have_ref[...].astype(F32)
    for n in range(groups):
        match = hot(rows_like((slots, block)) == slot - n * slots)
        total += dot_nn(moved_ref[n], match)
    out_ref[...] = total.astype(BF)


def embed_more(slot, moved, have):
    columns, count = have.shape
    block = min(512, count)
    return pl.pallas_call(
        more_kernel,
        grid=(count // block,),
        in_specs=[
            pl.BlockSpec((1, block), lambda i: (0, i)),
            pl.BlockSpec(moved.shape, lambda i: (0, 0, 0)),
            pl.BlockSpec((columns, block), lambda i: (0, i)),
        ],
        out_specs=pl.BlockSpec((columns, block), lambda i: (0, i)),
        out_shape=shape((columns, count), BF),
        compiler_params=params(),
        name="embed_more",
    )(slot, moved, have)


def bucket_kernel(slot_ref, near_ref, far_ref, out_ref):
    slots = out_ref.shape[2]
    half = near_ref.shape[1]
    start = pl.program_id(0) * slots
    match = hot(rows_like((slots, 2 * half)) == slot_ref[...] - start)
    total = dot_nt(near_ref[...], match[:, :half]) + dot_nt(far_ref[...], match[:, half:])
    out_ref[0] = total.astype(BF)


def bucket(slot, near, far, groups, slots):
    columns = near.shape[0]
    return pl.pallas_call(
        bucket_kernel,
        grid=(groups,),
        in_specs=[whole(slot.shape), whole(near.shape), whole(far.shape)],
        out_specs=pl.BlockSpec((1, columns, slots), lambda i: (i, 0, 0)),
        out_shape=shape((groups, columns, slots), BF),
        compiler_params=params(),
        cost_estimate=cost(0.2),
        name="bucket",
    )(slot, near, far)


def know_grad_kernel(where_ref, code_ref, *refs, base, parts):
    out_ref = refs[-1]
    size = out_ref.shape[2]
    count = code_ref.shape[1]
    step = pl.program_id(0)
    start = (where_ref[0] ^ (base + 4 * (step % 2) + step // 2)) * size
    first = start // KNOW
    last = (start + size - 1) // KNOW
    rows = rows_like((size, count)) + start
    match = rows == code_ref[pl.ds(first, 1), :] + first * KNOW
    match = match | (rows == code_ref[pl.ds(last, 1), :] + last * KNOW)
    match = hot(match)
    width = count // parts
    total = sum(dot_nt(refs[k][...], match[:, k * width : (k + 1) * width]) for k in range(parts))
    if len(refs) > parts + 1:
        total += refs[parts][0].astype(F32)
    out_ref[0] = total.astype(BF)


def know_grads(turned, codes, start, data, base, have):
    columns, count = data[0].shape
    size = TABLES * KNOW // SHARDS
    part = pl.BlockSpec((1, columns, size), lambda i, s: (i, 0, 0))
    return pl.pallas_call(
        partial(know_grad_kernel, base=base, parts=len(data)),
        grid_spec=pltpu.PrefetchScalarGridSpec(
            num_scalar_prefetch=1,
            grid=(4,),
            in_specs=[pl.BlockSpec((TABLES, count * len(data)), lambda i, s: (0, start))]
            + [whole(d.shape) for d in data]
            + [part] * len(have),
            out_specs=part,
        ),
        out_shape=shape((4, columns, size), BF),
        compiler_params=params(),
        cost_estimate=cost(0.2),
        name="know_grads",
    )(turned[None], codes, *data, *have)


def collect_kernel(list_ref, sent_ref, out_ref):
    groups, columns, slots = sent_ref.shape
    block = out_ref.shape[1]
    start = pl.program_id(0) * block
    total = jnp.zeros((columns, block), F32)
    for n in range(groups):
        match = hot(lanes_like((slots, block)) == list_ref[n] - start)
        total += dot_nn(sent_ref[n], match)
    out_ref[...] = total


def collect(lists, sent, owned):
    groups, columns, slots = sent.shape
    block = 512
    return pl.pallas_call(
        collect_kernel,
        grid=(pl.cdiv(owned, block),),
        in_specs=[
            pl.BlockSpec(lists.shape, lambda i: (0, 0, 0)),
            pl.BlockSpec(sent.shape, lambda i: (0, 0, 0)),
        ],
        out_specs=pl.BlockSpec((columns, block), lambda i: (0, i)),
        out_shape=shape((columns, owned), F32),
        compiler_params=params(),
        cost_estimate=cost(15),
        name="collect",
    )(lists, sent)


def add_know_kernel(where_ref, have_ref, *refs, order, window):
    know_refs, out_ref, table_ref = refs[:-2], refs[-2], refs[-1]
    columns, size = know_refs[0].shape
    step = pl.program_id(0)

    @pl.when(step == 0)
    def _():
        for k, know_ref in enumerate(know_refs):
            table_ref[:, order[k] * size : (order[k] + 1) * size] = know_ref[...]

    block = out_ref.shape[1]
    total = len(know_refs) * size
    origin = step * block - where_ref[0]
    base = jnp.clip((origin // 128) * 128, 0, total - window)
    base = pl.multiple_of(base, 128)
    part = table_ref[:, pl.ds(base, window)].astype(F32)
    turn = lax.rem(lax.rem(base - origin, window) + window, window)
    part = pltpu.roll(part, turn, 1)[:, :block]
    index = lanes_like((columns, block)) + origin
    out_ref[...] = have_ref[...] + jnp.where((index >= 0) & (index < total), part, 0.0)


def add_know(offset, have, know, order):
    columns, owned = have.shape
    block = 1024
    part = pl.BlockSpec((columns, block), lambda i, s: (0, i))
    return pl.pallas_call(
        partial(add_know_kernel, order=order, window=block + 128),
        grid_spec=pltpu.PrefetchScalarGridSpec(
            num_scalar_prefetch=1,
            grid=(pl.cdiv(owned, block),),
            in_specs=[part] + [pl.BlockSpec(k.shape, lambda i, s: (0, 0)) for k in know],
            out_specs=part,
            scratch_shapes=[pltpu.VMEM((columns, TABLES * KNOW), BF)],
        ),
        out_shape=shape((columns, owned), F32),
        input_output_aliases={1: 0},
        compiler_params=params(),
        cost_estimate=cost(0.2),
        name="add_know",
    )(offset[None], have, *know)


def collect_more_kernel(list_ref, sent_ref, have_ref, out_ref):
    groups, columns, slots = sent_ref.shape
    block = out_ref.shape[1]
    start = pl.program_id(0) * block
    total = have_ref[...]
    for n in range(groups):
        match = hot(lanes_like((slots, block)) == list_ref[n] - start)
        total += dot_nn(sent_ref[n], match)
    out_ref[...] = total


def collect_more(lists, sent, have):
    columns, owned = have.shape
    block = 512
    return pl.pallas_call(
        collect_more_kernel,
        grid=(pl.cdiv(owned, block),),
        in_specs=[
            pl.BlockSpec(lists.shape, lambda i: (0, 0, 0)),
            pl.BlockSpec(sent.shape, lambda i: (0, 0, 0)),
            pl.BlockSpec((columns, block), lambda i: (0, i)),
        ],
        out_specs=pl.BlockSpec((columns, block), lambda i: (0, i)),
        out_shape=shape((columns, owned), F32),
        compiler_params=params(),
        name="collect_more",
    )(lists, sent, have)


def project_kernel(where_ref, e0, e1, e2, e3, vec_ref, w_ref, bias_ref, f_ref, p_ref, col_ref):
    col_ref[...] = vec_ref[...].T
    pieces = [e[...].astype(F32) for e in (e0, e1, e2, e3)]
    part = pieces[0].shape[0]
    width = 4 * part
    average = sum(jnp.sum(p, 0, keepdims=True) for p in pieces) / width
    pieces = [p - average for p in pieces]
    spread = sum(jnp.sum(p * p, 0, keepdims=True) for p in pieces) / width
    scale = lax.rsqrt(spread + norm_eps)
    for j in range(4):
        rows = pl.ds(pl.multiple_of((where_ref[0] ^ j) * part, 64), part)
        unit = pieces[j] * scale
        f_ref[rows, :] = (unit * col_ref[rows, 0:1] + col_ref[rows, 1:2]).astype(BF)
    p_ref[...] = (dot_nn(w_ref[...], f_ref[...]) + bias_ref[...].T[:, 0:1]).astype(BF)


def project(place, pieces, vectors, weight, bias):
    part, count = pieces[0].shape
    block = count // 2

    def piece_spec(j):
        return pl.BlockSpec((part, block), lambda i, s: (0, i ^ (j & 1)))

    return pl.pallas_call(
        project_kernel,
        grid_spec=pltpu.PrefetchScalarGridSpec(
            num_scalar_prefetch=1,
            grid=(2,),
            in_specs=[piece_spec(j) for j in range(4)]
            + [whole(vectors.shape), whole(weight.shape), whole(bias.shape)],
            scratch_shapes=[pltpu.VMEM((4 * part, 8), F32)],
            out_specs=[
                pl.BlockSpec((4 * part, block), lambda i, s: (0, i)),
                pl.BlockSpec((weight.shape[0], block), lambda i, s: (0, i)),
            ],
        ),
        out_shape=[shape((4 * part, count), BF), shape((weight.shape[0], count), BF)],
        compiler_params=params(),
        cost_estimate=cost(4),
        name="project",
    )(place[None], *pieces, vectors, weight, bias)


def two_parts(value):
    high = value.astype(BF).astype(F32)
    return high, value - high


def widened(part, head, head_dim, extra):
    columns, count = part.shape
    rows = rows_like((columns, count))
    keep = (rows >= head * head_dim) & (rows < (head + 1) * head_dim)
    kept = jnp.where(keep, part, 0.0)
    below = rows_like((256 - columns, count))
    rest = jnp.zeros((256 - columns, count), F32)
    for at, row in enumerate(extra):
        rest = jnp.where(below == at, row, rest)
    return jnp.concatenate([kept, rest], 0).astype(BF)


def attend_kernel(
    q_ref, near_ref, far_ref, mask_ref, out_ref, lse_ref, keys_ref, values_ref, *, heads, head_dim
):
    columns = heads * head_dim
    half = near_ref.shape[1]
    count = 2 * half

    @pl.when(pl.program_id(0) == 0)
    def _():
        rest = rows_like((256 - columns, count))
        rest = jnp.where(rest == 0, mask_ref[...], 0.0)
        for at, ref in ((0, near_ref), (half, far_ref)):
            k = ref[columns : 2 * columns, :].astype(F32)
            k = jnp.concatenate([k, rest[:, at : at + half]], 0)
            keys_ref[at : at + half, :] = k.T.astype(BF)
            values_ref[:, at : at + half] = ref[2 * columns :, :]

    queries = q_ref[...].astype(F32) * head_dim ** (-0.5)
    ones = jnp.ones((1, queries.shape[1]), F32)
    for h in range(heads):
        scores = dot_nn(keys_ref[...], widened(queries, h, head_dim, [ones]))
        highest = jnp.max(scores, 0, keepdims=True)
        expanded = jnp.exp(scores - highest)
        total = jnp.sum(expanded, 0, keepdims=True)
        rows = slice(h * head_dim, (h + 1) * head_dim)
        out_ref[rows, :] = (dot_nn(values_ref[rows, :], expanded.astype(BF)) / total).astype(BF)
        lse_ref[h : h + 1, :] = highest + jnp.log(total)


def attend(near, far, mask, half, heads, head_dim):
    count = near.shape[1]
    columns = heads * head_dim
    block = 256
    return pl.pallas_call(
        partial(attend_kernel, heads=heads, head_dim=head_dim),
        grid=(count // block,),
        in_specs=[
            pl.BlockSpec((columns, block), lambda i: (0, i)),
            whole(near.shape),
            whole(far.shape),
            whole(mask.shape),
        ],
        out_specs=[
            pl.BlockSpec((columns, block), lambda i: (0, i)),
            pl.BlockSpec((8, block), lambda i: (0, i)),
        ],
        out_shape=[shape((columns, count), BF), shape((8, count), F32)],
        scratch_shapes=[pltpu.VMEM((2 * count, 256), BF), pltpu.VMEM((columns, 2 * count), BF)],
        compiler_params=params(),
        cost_estimate=cost(16),
        name="attend",
    )((near, far)[half], near, far, mask)


def attend_back_kernel(
    near_ref, far_ref, mask_ref, o_near, o_far, g_ref, lse_near, lse_far, d_ref,
    keys_ref, values_ref, flat_ref, q_ref, o_ref, lse_ref, dk_acc, dv_acc, *, heads, head_dim,
):
    step = pl.program_id(0)
    columns = heads * head_dim
    half = near_ref.shape[1]
    count = 2 * half
    block = g_ref.shape[1]
    steps = half // block

    @pl.when(step < steps)
    def _():
        at = pl.ds(pl.multiple_of(step * block, 128), block)
        q_ref[...] = near_ref[:columns, at]
        o_ref[...] = o_near[:, at]
        lse_ref[...] = lse_near[:, at]

    @pl.when(step >= steps)
    def _():
        at = pl.ds(pl.multiple_of((step - steps) * block, 128), block)
        q_ref[...] = far_ref[:columns, at]
        o_ref[...] = o_far[:, at]
        lse_ref[...] = lse_far[:, at]

    @pl.when(step == 0)
    def _():
        rest = rows_like((256 - columns, count))
        ones = jnp.where((rest == 1) | (rest == 2), 1.0, 0.0)
        with_mask = jnp.where(rest == 0, mask_ref[...], ones)
        for at, ref in ((0, near_ref), (half, far_ref)):
            part = slice(at, at + half)
            k = ref[columns : 2 * columns, :]
            v = ref[2 * columns :, :].astype(F32)
            flat_ref[:, part] = k
            k = jnp.concatenate([k.astype(F32), with_mask[:, part]], 0)
            keys_ref[part, :] = k.T.astype(BF)
            values_ref[part, :] = jnp.concatenate([v, ones[:, part]], 0).T.astype(BF)
        dk_acc[...] = jnp.zeros_like(dk_acc)
        dv_acc[...] = jnp.zeros_like(dv_acc)

    score_scale = head_dim ** (-0.5)
    queries = q_ref[...].astype(F32) * score_scale
    grads = g_ref[...].astype(F32)
    inner = grads * o_ref[...].astype(F32)
    by_query = queries.T
    by_grad = grads.T
    lanes = lanes_like(by_query.shape)
    one = jnp.ones((1, block), F32)
    zero = jnp.zeros((1, block), F32)
    here = pl.ds(pl.multiple_of(step * block, 128), block)
    for h in range(heads):
        rows = slice(h * head_dim, (h + 1) * head_dim)
        keep = (lanes >= h * head_dim) & (lanes < (h + 1) * head_dim)
        lse = two_parts(-lse_ref[h : h + 1, :])
        delta = two_parts(-jnp.sum(inner[rows, :], 0, keepdims=True))
        scores = dot_nn(keys_ref[...], widened(queries, h, head_dim, [one, *lse]))
        probs = jnp.exp(scores)
        dv_acc[...] += dot_nn(probs.astype(BF), jnp.where(keep, by_grad, 0.0).astype(BF))
        grad_probs = dot_nn(values_ref[...], widened(grads, h, head_dim, [zero, *delta]))
        grad_scores = (probs * grad_probs).astype(BF)
        dk_acc[...] += dot_nn(grad_scores, jnp.where(keep, by_query, 0.0).astype(BF))
        d_ref[rows, here] = (dot_nn(flat_ref[rows, :], grad_scores) * score_scale).astype(BF)

    @pl.when(step == pl.num_programs(0) - 1)
    def _():
        d_ref[columns : 2 * columns, :] = dk_acc[...].T.astype(BF)
        d_ref[2 * columns :, :] = dv_acc[...].T.astype(BF)


def attend_back(near, far, mask, out, grad, lse, heads, head_dim):
    rows, half = near.shape
    count = 2 * half
    columns = heads * head_dim
    block = 256
    arrays = (near, far, mask, *out, grad, *lse)
    specs = [whole(a.shape) for a in arrays]
    specs[5] = pl.BlockSpec((columns, block), lambda i: (0, i))
    return pl.pallas_call(
        partial(attend_back_kernel, heads=heads, head_dim=head_dim),
        grid=(count // block,),
        in_specs=specs,
        out_specs=whole((rows, count)),
        out_shape=shape((rows, count), BF),
        scratch_shapes=[
            pltpu.VMEM((count, 256), BF),
            pltpu.VMEM((count, 256), BF),
            pltpu.VMEM((columns, count), BF),
            pltpu.VMEM((columns, block), BF),
            pltpu.VMEM((columns, block), BF),
            pltpu.VMEM((8, block), F32),
            pltpu.VMEM((count, columns), F32),
            pltpu.VMEM((count, columns), F32),
        ],
        compiler_params=params(),
        cost_estimate=cost(38),
        name="attend_back",
    )(*arrays)


def to_second_kernel(where_ref, *refs):
    h_refs, e_refs, o_refs = refs[0:4], refs[4:8], refs[8:12]
    vec_ref, resid_ref, upper_ref, lower_ref, emb_ref = refs[12:]
    part = h_refs[0].shape[0]
    for j in range(4):
        rows = pl.ds(pl.multiple_of((where_ref[0] ^ j) * part, 64), part)
        emb_ref[rows, :] = e_refs[j][...].astype(F32)
    resid = emb_ref[...].T + vec_ref[0:1, :]
    for j in range(4):
        resid += dot_tn(h_refs[j][...], o_refs[j][...])
    resid_ref[...] = resid
    centered = resid - jnp.mean(resid, -1, keepdims=True)
    spread = jnp.mean(centered * centered, -1, keepdims=True)
    unit = centered * lax.rsqrt(spread + norm_eps)
    second = (unit * vec_ref[1:2, :] + vec_ref[2:3, :]).astype(BF)
    half = second.shape[0] // 2
    upper_ref[...] = second[:half]
    lower_ref[...] = second[half:]


def to_second(place, heads, pieces, outs, vectors):
    part, count = heads[0].shape
    width = outs[0].shape[1]

    def piece_spec(j):
        return pl.BlockSpec((part, count), lambda i, s: (0, j & 1))

    return pl.pallas_call(
        to_second_kernel,
        grid_spec=pltpu.PrefetchScalarGridSpec(
            num_scalar_prefetch=1,
            grid=(1,),
            in_specs=[whole((part, count))] * 4
            + [piece_spec(j) for j in range(4)]
            + [whole(w.shape) for w in outs]
            + [whole(vectors.shape)],
            out_specs=[whole((count, width))] + [whole((count // 2, width))] * 2,
            scratch_shapes=[pltpu.VMEM((width, count), F32)],
        ),
        out_shape=[shape((count, width), F32)] + [shape((count // 2, width), BF)] * 2,
        compiler_params=params(),
        cost_estimate=cost(4),
        name="to_second",
    )(place[None], *heads, *pieces, *outs, vectors)


def feed_kernel(s0, s1, g0, g1, up_ref, down_ref, bias_ref, *outs):
    for k, (second_ref, g_ref) in enumerate(((s0, g0), (s1, g1))):
        act_ref, pre_ref, grad_ref = outs[3 * k : 3 * k + 3]
        pre_act = dot_nn(second_ref[...], up_ref[...]) + bias_ref[...]
        inside = 0.5 * (1.0 + lax.erf(pre_act * (0.5**0.5)))
        density = jnp.exp(-0.5 * pre_act * pre_act) * 0.3989422804014327
        act_ref[...] = (pre_act * inside).astype(BF)
        grad_act = dot_nt(g_ref[...], down_ref[...])
        grad_pre = (grad_act * (inside + pre_act * density)).astype(BF)
        pre_ref[...] = grad_pre
        grad_ref[...] = dot_nt(grad_pre, up_ref[...]).astype(BF)


def feed_pair(seconds, grad_outs, up, down, bias):
    count, width = seconds[0].shape
    units = up.shape[1]
    arrays = (*seconds, *grad_outs, up, down, bias)
    unit, token = shape((count, units), BF), shape((count, width), BF)
    found = pl.pallas_call(
        feed_kernel,
        grid=(1,),
        in_specs=[whole(a.shape) for a in arrays],
        out_specs=[whole(a.shape) for a in (unit, unit, token) * 2],
        out_shape=[unit, unit, token] * 2,
        compiler_params=params(),
        cost_estimate=cost(5),
        name="feed_pair",
    )(*arrays)
    return found[:3], found[3:]


def rows_of(refs):
    return jnp.concatenate([r[...] for r in refs], 0)


def feed_weight_kernel(*refs):
    s_refs, p_refs, a_refs, g_refs = refs[0:8], refs[8:16], refs[16:24], refs[24:32]
    out_ref, sum_ref = refs[32:]
    up = dot_tn(rows_of(s_refs), rows_of(p_refs))
    out_ref[0] = up.astype(BF)
    down = dot_tn(rows_of(a_refs), rows_of(g_refs))
    out_ref[1] = down.astype(BF)
    total = sum(jnp.sum(p[...].astype(F32), 0, keepdims=True) for p in p_refs)
    sum_ref[...] = jnp.broadcast_to(total, sum_ref.shape)


def feed_weights(seconds, grad_pres, activated, grad_outs):
    width, units = seconds[0].shape[1], grad_pres[0].shape[1]
    arrays = (*seconds, *grad_pres, *activated, *grad_outs)
    return pl.pallas_call(
        feed_weight_kernel,
        grid=(1,),
        in_specs=[whole(a.shape) for a in arrays],
        out_specs=[whole((2, width, units)), whole((8, units))],
        out_shape=[shape((2, width, units), BF), shape((8, units), F32)],
        compiler_params=params(),
        cost_estimate=cost(9),
        name="feed_weights",
    )(*arrays)


def to_heads_kernel(resid_ref, a0, a1, b0, b1, c0, c1, g0, g1, *refs):
    o_refs = refs[0:4]
    vec_ref, low_ref, grad_ref, heads_ref, sums_ref = refs[4:]
    resid = resid_ref[...]
    centered = resid - jnp.mean(resid, -1, keepdims=True)
    spread = jnp.mean(centered * centered, -1, keepdims=True)
    scale = lax.rsqrt(spread + norm_eps)
    unit = centered * scale
    grad_second = sum(rows_of(pair).astype(F32) for pair in ((a0, a1), (b0, b1), (c0, c1)))
    e = grad_second * vec_ref[1:2, :]
    first_mean = jnp.mean(e, -1, keepdims=True)
    second_mean = jnp.mean(e * unit, -1, keepdims=True)
    grad_out = rows_of((g0, g1)).astype(F32)
    grad_resid = grad_out + scale * (e - first_mean - unit * second_mean)
    low = grad_resid.astype(BF)
    low_ref[...] = low
    grad_ref[...] = grad_resid.T
    for j in range(4):
        heads_ref[j] = dot_nt(o_refs[j][...], low).astype(BF)
    rows = [grad_second * unit, grad_second, grad_resid, grad_out]
    rows = [jnp.sum(r, 0, keepdims=True) for r in rows]
    blank = jnp.zeros_like(rows[0])

    sums_ref[...] = jnp.concatenate(rows + [blank] * 4, 0)


def to_heads(resid, terms, grad_outs, outs, vectors):
    count, width = resid.shape
    part = outs[0].shape[0]
    token = whole((count, width))
    arrays = (resid, *terms, *grad_outs, *outs, vectors)
    return pl.pallas_call(
        to_heads_kernel,
        grid=(1,),
        in_specs=[whole(a.shape) for a in arrays],
        out_specs=[token, whole((width, count)), whole((4, part, count)), whole((8, width))],
        out_shape=[
            shape((count, width), BF),
            shape((width, count), F32),
            shape((4, part, count), BF),
            shape((8, width), F32),
        ],
        compiler_params=params(),
        cost_estimate=cost(6),
        name="to_heads",
    )(*arrays)


def rest_kernel(near_ref, far_ref, l0, l1, l2, l3, back_ref, f_near, f_far, out_ref):
    columns, half = near_ref.shape
    quarter = half // 2
    total = dot_nn(near_ref[:, :quarter], l0[...]) + dot_nn(near_ref[:, quarter:], l1[...])
    total += dot_nn(far_ref[:, :quarter], l2[...]) + dot_nn(far_ref[:, quarter:], l3[...])
    out_ref[:columns, :] = total.astype(BF)
    total = dot_nt(back_ref[:, :half], f_near[...]) + dot_nt(back_ref[:, half:], f_far[...])
    out_ref[columns:, :] = total.astype(BF)


def rest_weights(near, far, lows, back, firsts):
    width = firsts[0].shape[0]
    arrays = (near, far, *lows, back, *firsts)
    dims = (near.shape[0] + back.shape[0], width)
    return pl.pallas_call(
        rest_kernel,
        grid=(1,),
        in_specs=[whole(a.shape) for a in arrays],
        out_specs=whole(dims),
        out_shape=shape(dims, BF),
        compiler_params=params(),
        cost_estimate=cost(6),
        name="rest_weights",
    )(*arrays)


def back_kernel(back_ref, w_ref, *outs):
    for j, out_ref in enumerate(outs):
        count = out_ref.shape[1]
        rows = back_ref[:, j * count : (j + 1) * count]
        out_ref[...] = dot_nn(w_ref[...], rows).astype(BF)


def first_grads(back, weight):
    count = back.shape[1] // 4
    width = weight.shape[0]
    return pl.pallas_call(
        back_kernel,
        grid=(1,),
        in_specs=[whole(back.shape), whole(weight.shape)],
        out_specs=[whole((width, count))] * 4,
        out_shape=[shape((width, count), BF)] * 4,
        compiler_params=params(),
        cost_estimate=cost(3),
        name="first_grads",
    )(back, weight)


def finish_kernel(
    where_ref, a_ref, b_ref, c_ref, e0, e1, e2, e3, resid_ref, vec_ref,
    cols_ref, rows_ref, sums_ref, emb_ref,
):
    part = e0.shape[0]
    width = 4 * part
    for j, e in enumerate((e0, e1, e2, e3)):
        rows = pl.ds(pl.multiple_of((where_ref[0] ^ j) * part, 64), part)
        emb_ref[rows, :] = e[...].astype(F32)
    grad = a_ref[...].astype(F32) + b_ref[...].astype(F32) + c_ref[...].astype(F32)
    values = emb_ref[...]
    centered = values - jnp.sum(values, 0, keepdims=True) / width
    spread = jnp.sum(centered * centered, 0, keepdims=True) / width
    scale = lax.rsqrt(spread + norm_eps)
    unit = centered * scale
    e = grad * vec_ref[...].T[:, 0:1]
    first_mean = jnp.sum(e, 0, keepdims=True) / width
    second_mean = jnp.sum(e * unit, 0, keepdims=True) / width
    total = resid_ref[...] + scale * (e - first_mean - unit * second_mean)
    emb_ref[...] = total
    for j in range(4):
        rows = pl.ds(pl.multiple_of((where_ref[0] ^ j) * part, 64), part)
        cols_ref[j] = emb_ref[rows, :].astype(BF)
    rows_ref[...] = total.T.astype(BF)
    sums_ref[:, 0:1] = jnp.sum(grad * unit, 1, keepdims=True)
    sums_ref[:, 1:2] = jnp.sum(grad, 1, keepdims=True)


def finish(place, a, b, c, pieces, resid, vectors):
    width, count = a.shape
    part = pieces[0].shape[0]

    def piece_spec(j):
        return pl.BlockSpec((part, count), lambda i, s: (0, j & 1))

    return pl.pallas_call(
        finish_kernel,
        grid_spec=pltpu.PrefetchScalarGridSpec(
            num_scalar_prefetch=1,
            grid=(1,),
            in_specs=[whole(a.shape)] * 3
            + [piece_spec(j) for j in range(4)]
            + [whole(resid.shape), whole(vectors.shape)],
            out_specs=[whole((4, part, count)), whole((count, width)), whole((width, 128))],
            scratch_shapes=[pltpu.VMEM((width, count), F32)],
        ),
        out_shape=[
            shape((4, part, count), BF),
            shape((count, width), BF),
            shape((width, 128), F32),
        ],
        compiler_params=params(),
        cost_estimate=cost(4),
        name="finish",
    )(place[None], a, b, c, *pieces, resid, vectors)


def body(
    gene_ids,
    know_ids,
    lengths,
    tables,
    norm_gain,
    norm_bias,
    qkv_weight,
    qv_bias,
    out_weight,
    out_bias,
    up_weight,
    up_bias,
    down_weight,
    down_bias,
    cotangent,
):
    count = gene_ids.shape[0]
    width = norm_gain.shape[1]
    columns = qkv_weight.shape[2]
    units = up_weight.shape[1]
    head_dim = width // HEADS
    heads_here = columns // head_dim
    owned = tables.shape[0]
    groups = lax.axis_size("dp")
    place = lax.axis_index("tensor")
    group = lax.axis_index("dp")
    quarter = count // 4
    length = lengths[0]
    slots = 128 * (-(-(3 * count // (2 * groups)) // 128))
    know_rows = TABLES * KNOW
    share = know_rows // SHARDS
    start = VOCAB - (groups - 1) * owned
    one_owner = start >= 0 and groups == SHARDS

    def block_at(value, j, size, axis=0):
        return lax.dynamic_slice_in_dim(value, (place ^ j) * size, size, axis)

    def relative(value, size, axis=0):
        return jnp.concatenate([block_at(value, j, size, axis) for j in range(4)], axis)

    ids = relative(gene_ids, quarter)[None]
    codes = relative(know_ids, quarter, 1)
    step = 1
    while step < groups:
        ids = jnp.concatenate([ids, hop(ids, "dp", step)], 0)
        step *= 2
    lists, slot, most = route(group, jnp.int32(0), ids, owned, slots)
    rounds = (most[0, 0] + slots - 1) // slots

    table = tables.T

    picked = pick(lists, table)

    if one_owner:
        held = after(table, ids)[:, start : start + know_rows]
        shards = [held[:, i * share : (i + 1) * share] for i in range(SHARDS)]
        dealt = [lax.ppermute(shards[i], "dp", [(groups - 1, i)]) for i in range(groups - 1)]
        mine = jnp.where(group == groups - 1, shards[-1], jnp.zeros((), BF))
        mine = sum(after(dealt, picked), mine)
        know, order = mine[None], (0,)
        for step in (4, 2, 1):
            know = jnp.concatenate([know, hop(know, "dp", step)], 0)
            order = order + tuple(k | step for k in order)
        turned = group
    else:
        room = jnp.pad(table, ((0, 0), (know_rows, know_rows)))
        begin = jnp.clip(VOCAB - group * owned + know_rows, 0, owned + know_rows)
        know = lax.psum(lax.dynamic_slice_in_dim(room, begin, know_rows, 1), "dp")
        know = jnp.stack([know[:, i * share : (i + 1) * share] for i in range(SHARDS)])
        turned = jnp.int32(0)
        order = tuple(range(SHARDS))

    def exchange(blocks):
        return lax.all_to_all(blocks, "dp", 0, 0, tiled=True)

    def more_rows(carry):
        turn, total = carry
        these, at, _ = route(group, turn, ids, owned, slots)
        return turn + 1, embed_more(at, exchange(pick(these, table)), total)

    blank = jnp.zeros((columns, count), BF)
    _, extra = lax.while_loop(lambda c: c[0] < rounds, more_rows, (jnp.int32(1), blank))

    out_blocks = gather_four(out_weight)
    moved = exchange(picked)
    moved = after(moved, extra, *out_blocks)

    own = [embed(0, turned, order, slot, codes, moved, know, extra)]
    far = [hop(own[0], "tensor", 2)]
    own.append(embed(1, turned, order, slot, codes, after(moved, own[0]), know, extra))
    far.append(hop(after(own[1], far[0]), "tensor", 2))
    near = [hop(o, "tensor", 1) for o in own]
    third = [hop(far[0], "tensor", 1)]

    gain = norm_gain.astype(F32)
    shift = norm_bias.astype(F32)
    weight = qkv_weight.transpose(0, 2, 1).reshape(3 * columns, width)
    weight_down = weight.T
    bias = qv_bias.astype(F32)
    bias = jnp.concatenate([bias[0], jnp.zeros((columns,), F32), bias[1]])[None]
    bias = jnp.pad(bias, ((0, 7), (0, 0)))
    norm_rows = jnp.pad(jnp.stack([gain[0], shift[0]]), ((0, 6), (0, 0)))
    upper = (own[1], near[1], far[0], third[0])
    upper = project(place, upper, norm_rows, weight, bias)
    far[1] = after(far[1], upper)
    third.append(hop(far[1], "tensor", 1))
    lower = (own[0], near[0], far[1], third[1])
    halves = project(place, lower, norm_rows, weight, bias), upper
    pieces = (own[0], near[0], far[1], third[1])
    firsts, projected = zip(*halves)
    spots = relative(jnp.arange(count, dtype=I32), quarter)
    mask = jnp.where(spots < length, 0.0, -1e30).astype(F32)[None]
    valid = jnp.arange(count, dtype=I32) < length
    grad_full = cotangent * valid[:, None].astype(BF)
    eighth = quarter // 2
    grad_outs = []
    for j in range(4):
        rows = block_at(grad_full, j, quarter)
        grad_outs.append((rows[:eighth], rows[eighth:]))
    far_heads, far_lse = attend(*projected, after(mask, grad_outs, weight_down), 1, heads_here, head_dim)
    near_heads, near_lse = attend(*projected, after(mask, far_heads), 0, heads_here, head_dim)

    from_far = [hop(far_heads[:, k * quarter :][:, :quarter], "tensor", 2 + k) for k in (0, 1)]
    near_heads = after(near_heads, from_far)
    heads = [near_heads[:, :quarter], hop(near_heads[:, quarter:], "tensor", 1), *from_far]
    vectors = jnp.stack([out_bias.astype(F32), gain[1], shift[1]])
    up_row = up_bias.astype(F32)[None]

    def feed(rows, grads):
        return feed_pair(rows, grads, up_weight, down_weight, up_row)

    resid, *second = to_second(place, heads, pieces, out_blocks, vectors)
    beside = [hop(s, "tensor", 1) for s in second]
    across = [hop(s, "tensor", 2) for s in second]
    own_blocks = feed(second, grad_outs[0])
    near_blocks = feed(beside, grad_outs[1])
    blocks = [own_blocks, near_blocks]
    seconds, terms = [second, beside], []
    for half in (0, 1):
        rows = after(across[half], blocks)
        rows = [rows, hop(rows, "tensor", 1)]
        found = feed(rows, (grad_outs[2][half], grad_outs[3][half]))
        two = (found[0][2].astype(F32) + hop(found[1][2], "tensor", 1).astype(F32)).astype(BF)
        if half:
            two = after(two, terms[0])
        terms.append(hop(two, "tensor", 2))
        seconds.append(rows)
        blocks.append(found)
    pairs = [grad_outs[0], grad_outs[1]]
    pairs += [(grad_outs[2][k], grad_outs[3][k]) for k in (0, 1)]
    flat = [block for found in blocks for block in found]
    feed_part, unit_sums = feed_weights(
        [rows for pair in seconds for rows in pair],
        [f[1] for f in flat],
        [f[0] for f in flat],
        after([g for pair in pairs for g in pair], two),
    )
    low, grad_resid, grad_heads, sums = to_heads(
        resid,
        after(
            (
                *[f[2] for f in own_blocks],
                *[hop(f[2], "tensor", 1) for f in near_blocks],
                *terms,
            ),
            feed_part,
        ),
        grad_outs[0],
        out_blocks,
        vectors,
    )
    grads = jnp.concatenate(swap_four([grad_heads[j] for j in range(4)]), 1)
    low = after(low, grads)
    lows = swap_four([low] * 4)
    back = attend_back(
        *projected,
        mask,
        (near_heads, far_heads),
        grads,
        (near_lse, far_lse),
        heads_here,
        head_dim,
    )

    def sum_four(parts):
        two = parts[2].astype(F32) + hop(parts[3], "tensor", 1).astype(F32)
        zero = parts[0].astype(F32) + hop(parts[1], "tensor", 1).astype(F32)
        return zero + hop(two.astype(BF), "tensor", 2).astype(F32)

    feed_grad = lax.psum(feed_part, "dp")

    back = after(back, *lows)

    first_grad = first_grads(back, weight_down)

    two = first_grad[2].astype(F32) + hop(first_grad[3], "tensor", 1).astype(F32)
    back_later = after(back, two)
    rest = rest_weights(near_heads, far_heads, lows, back_later, firsts)
    acts = [own_blocks, near_blocks] + [[blocks[2][k], blocks[3][k]] for k in (0, 1)]
    feeds = []
    for pair in acts:
        rows = jnp.concatenate([found[0] for found in pair], 0)
        feeds.append(dot_nn(after(rows, rest), down_weight).astype(BF))
    from_far = hop(two.astype(BF), "tensor", 2)
    from_near = hop(first_grad[1], "tensor", 1)
    by_column, by_row, first_sums = finish(
        place,
        first_grad[0],
        from_near,
        from_far,
        pieces,
        grad_resid,
        norm_rows,
    )
    swapped = swap_four([by_column[j] for j in range(4)])
    near_columns = jnp.concatenate(swapped[:2], 1)
    far_columns = jnp.concatenate(swapped[2:], 1)

    odd_part = know_grads(turned, codes, 0, [near_columns], 2, ())
    far_columns = after(far_columns, odd_part)
    dealt = bucket(slot, near_columns, far_columns, groups, slots)
    sent = exchange(dealt)
    odd_part = know_grads(turned, after(codes, dealt), 1, [far_columns], 2, (odd_part,))
    both = [near_columns, far_columns]
    even_part = know_grads(turned, after(codes, odd_part, feed_grad), 0, both, 0, ())

    def halve(part):
        return part[:2].astype(F32), hop(part[2:], "dp", 1)

    if one_owner:
        odd_own, odd_other = halve(odd_part)
        odd_sum = (odd_own + odd_other.astype(F32)).astype(BF)
        even_own, even_other = halve(even_part)
        rest = lax.psum(rest, "dp", axis_index_groups=[list(range(groups))[::-1]])
        odd_far = hop(after(odd_sum, sent), "dp", 2)
    else:
        rest = lax.psum(after(rest, feed_grad), "dp")
    downs = after(lists, firsts).transpose(0, 2, 1)
    tables_grad = collect(downs, sent, owned)
    if one_owner:
        even_sum = even_own + even_other.astype(F32) + odd_far.astype(F32)
        know_sum = even_sum[0] + hop(even_sum[1].astype(BF), "dp", 4).astype(F32)
        know_sum = after(know_sum.astype(BF), tables_grad)
        last = jnp.where(group == groups - 1, know_sum, jnp.zeros((), BF))
        know_all = [lax.ppermute(know_sum, "dp", [(i, groups - 1)]) for i in range(groups - 1)]
        know_all, order = know_all + [last], tuple(range(SHARDS))
    else:
        know_all = lax.psum(jnp.concatenate([even_part, odd_part], 0), "dp")
        know_sum = know_all
        know_all, order = [know_all[k] for k in range(SHARDS)], (0, 4, 1, 5, 2, 6, 3, 7)

    def more_grads(carry):
        turn, total = carry
        these, at, _ = route(group, turn, ids, owned, slots)
        these = these.transpose(0, 2, 1)
        return turn + 1, collect_more(
            these, exchange(bucket(at, near_columns, far_columns, groups, slots)), total
        )

    _, tables_grad = lax.while_loop(
        lambda c: c[0] < rounds, more_grads, (jnp.int32(1), tables_grad)
    )

    feeds = after(feeds, far_columns)
    out_own = (resid + sum_four(feeds) + down_bias.astype(F32)).astype(BF)

    def spread_rows(own, kind):
        full = jnp.zeros((count, width), kind)
        for j, block in enumerate(gather_four(own)):
            full = lax.dynamic_update_slice_in_dim(
                full, block.astype(kind), (place ^ j) * quarter, 0
            )
        return full

    out = spread_rows(after(out_own, far_columns), BF)
    input_grad = spread_rows(after(by_row, far_columns), F32)

    feed_grad = after(feed_grad, sent).astype(F32)

    qv = jnp.sum(back.reshape(3, columns, count).astype(F32), -1)
    qv = jnp.stack([qv[0], qv[2]])
    qv_wide = lax.dynamic_update_slice_in_dim(
        jnp.zeros((2, width), F32), qv, place * columns, 1
    )
    up_sums = lax.dynamic_update_slice_in_dim(
        jnp.zeros((4, units), F32), unit_sums[0:1], place, 0
    )
    packed = jnp.concatenate(
        [
            first_sums[:, 0],
            first_sums[:, 1],
            sums[0:4].reshape(-1),
            qv_wide.reshape(-1),
            up_sums.reshape(-1),
        ]
    ).reshape(-1, 128)
    packed = after(packed, know_sum)
    for step in (1, 2):
        packed = packed + hop(packed, "tensor", step)
    step = 1
    while step < groups:
        packed = packed + hop(packed, "dp", step)
        step *= 2
    packed = packed.reshape(-1)
    know_all = after(know_all, packed, out, input_grad, feed_grad, rest)
    tables_grad = add_know(VOCAB - group * owned, tables_grad, know_all, order)
    rest = after(rest, tables_grad).astype(F32)
    outw_grad = rest[:columns]
    qkv_grad = rest[columns:].reshape(3, columns, width).transpose(0, 2, 1)
    tops = packed[: 6 * width].reshape(6, width)
    qv_wide = packed[6 * width : 8 * width].reshape(2, width)
    up_sums = packed[8 * width :].reshape(4, units)
    return (
        out,
        input_grad,
        tables_grad.T,
        jnp.stack([tops[0], tops[2]]),
        jnp.stack([tops[1], tops[3]]),
        qkv_grad,
        lax.dynamic_slice_in_dim(qv_wide, place * columns, columns, 1),
        outw_grad,
        tops[4],
        feed_grad[0],
        lax.dynamic_slice_in_dim(up_sums, place, 1, 0)[0],
        feed_grad[1],
        tops[5],
    )


def solution(mesh):
    placed = (
        P("dp"),
        P(None, "dp"),
        P("dp"),
        P("dp", "tensor"),
        P(),
        P(),
        P(None, None, "tensor"),
        P(None, "tensor"),
        P("tensor", None),
        P(),
        P(None, "tensor"),
        P("tensor"),
        P("tensor", None),
        P(),
        P("dp", None),
    )
    return jax.shard_map(
        body,
        mesh=mesh,
        in_specs=placed,
        out_specs=(
            P("dp", None),
            P("dp", None),
            P("dp", "tensor"),
            P(),
            P(),
            P(None, None, "tensor"),
            P(None, "tensor"),
            P("tensor", None),
            P(),
            P(None, "tensor"),
            P("tensor"),
            P("tensor", None),
            P(),
        ),
        check_vma=False,
    )
```

```python
from functools import partial

import jax
import jax.numpy as jnp
from jax import lax
from jax.experimental import pallas as pl
from jax.experimental.pallas import tpu as pltpu
from jax.sharding import PartitionSpec as P

HEADS = 12
VOCAB = 36000
KNOW = 1024
TABLES = 5
SHARDS = 8
norm_eps = 1e-05
BF = jnp.bfloat16
F32 = jnp.float32
I32 = jnp.int32
BIG = 56 * 1024 * 1024


def params():
    return pltpu.CompilerParams(vmem_limit_bytes=BIG)


def cost(micros):
    return pl.CostEstimate(
        flops=int(micros * 9e8), bytes_accessed=int(micros * 3e6), transcendentals=0
    )


def shape(dims, kind):
    return jax.ShapeDtypeStruct(dims, kind)


def dot_nt(left, right):
    return lax.dot_general(left, right, (((1,), (1,)), ((), ())), preferred_element_type=F32)


def dot_tn(left, right):
    return lax.dot_general(left, right, (((0,), (0,)), ((), ())), preferred_element_type=F32)


def dot_nn(left, right):
    return jnp.dot(left, right, preferred_element_type=F32)


def whole(dims):
    return pl.BlockSpec(dims, lambda i, *s: (0,) * len(dims))


def hot(condition):
    return condition.astype(F32).astype(BF)


def rows_like(dims):
    return lax.broadcasted_iota(I32, dims, 0)


def lanes_like(dims):
    return lax.broadcasted_iota(I32, dims, 1)


def after(value, *others):
    return lax.optimization_barrier((value, others))[0]


def hop(value, axis, flip):
    count = lax.axis_size(axis)
    return lax.ppermute(value, axis, [(i, i ^ flip) for i in range(count)])


def gather_four(block):
    far = hop(block, "tensor", 2)
    return [block, hop(block, "tensor", 1), far, hop(far, "tensor", 1)]


def swap_four(pieces):
    return [pieces[0]] + [hop(pieces[j], "tensor", j) for j in (1, 2, 3)]


def route_kernel(where_ref, ids_ref, lists_ref, slot_ref, most_ref, *, owned, slots):
    group, turn = where_ref[0], where_ref[1]
    ids = ids_ref[...]
    groups, count = ids.shape
    wanted = (ids >= group * owned) & (ids < (group + 1) * owned)
    mine = jnp.broadcast_to(ids[0:1, :], (groups, count))
    owners = rows_like((groups, count))
    held = (mine >= owners * owned) & (mine < (owners + 1) * owned)
    flags = jnp.concatenate([wanted.astype(F32), held.astype(F32)], 0)
    sums = flags
    lanes = lanes_like(flags.shape)
    step = 1
    while step < count:
        sums = sums + jnp.where(lanes >= step, pltpu.roll(sums, step, 1), 0.0)
        step *= 2
    low = (turn * slots).astype(F32)
    ranks = sums[:groups] - 1.0 - low
    ranks = jnp.where(wanted & (ranks >= 0.0) & (ranks < slots), ranks, -1.0).astype(I32)
    plus = jnp.where(wanted, ids - group * owned + 1, 0)
    spots = rows_like((slots, count))
    halves = rows_like((16, count))
    for k in range(groups):
        number = jnp.broadcast_to(plus[k : k + 1, :], (16, count))
        parts = jnp.where(halves == 0, number >> 8, jnp.where(halves == 1, number & 255, 0))
        parts = parts.astype(F32).astype(BF)
        match = hot(spots == ranks[k : k + 1, :])
        found = dot_nt(parts, match)
        lists_ref[group ^ k] = (found[0:1, :] * 256.0 + found[1:2, :]).astype(I32) - 1
    own = sums[groups:] - 1.0 - low
    good = held & (own >= 0.0) & (own < slots)
    slot = jnp.where(good, owners.astype(F32) * slots + own + 1.0, 0.0)
    slot = jnp.sum(slot, 0, keepdims=True) - 1.0
    slot_ref[...] = slot.astype(I32)
    most = jnp.zeros((groups, 1), F32)
    for o in range(groups):
        here = (ids >= o * owned) & (ids < (o + 1) * owned)
        most = jnp.maximum(most, jnp.sum(here.astype(F32), 1, keepdims=True))
    most_ref[...] = jnp.broadcast_to(jnp.max(most, 0, keepdims=True), (8, 128)).astype(I32)


def route(group, turn, ids, owned, slots):
    groups, count = ids.shape

    return pl.pallas_call(
        partial(route_kernel, owned=owned, slots=slots),
        grid_spec=pltpu.PrefetchScalarGridSpec(
            num_scalar_prefetch=1,
            grid=(1,),
            in_specs=[whole(ids.shape)],
            out_specs=[
                whole((groups, 1, slots)),
                whole((1, count)),
                whole((8, 128)),
            ],
        ),
        out_shape=[
            shape((groups, 1, slots), I32),
            shape((1, count), I32),
            shape((8, 128), I32),
        ],
        compiler_params=params(),
        cost_estimate=cost(8),
        name="route",
    )(jnp.stack([group, turn]), ids)


def pick_kernel(list_ref, table_ref, out_ref, *, chunk):
    wanted = list_ref[0]
    size = table_ref.shape[1]
    total = jnp.zeros(out_ref.shape[1:], F32)
    for start in range(0, size, chunk):
        part = min(chunk, size - start)
        match = hot(rows_like((part, wanted.shape[1])) == wanted - start)
        total += dot_nn(table_ref[:, start : start + part], match)
    out_ref[0] = total.astype(BF)


def pick(lists, table):
    groups, _, slots = lists.shape
    columns = table.shape[0]
    return pl.pallas_call(
        partial(pick_kernel, chunk=512),
        grid=(groups,),
        in_specs=[
            pl.BlockSpec((1, 1, slots), lambda i: (i, 0, 0)),
            pl.BlockSpec(table.shape, lambda i: (0, 0)),
        ],
        out_specs=pl.BlockSpec((1, columns, slots), lambda i: (i, 0, 0)),
        out_shape=shape((groups, columns, slots), BF),
        compiler_params=params(),
        cost_estimate=cost(12),
        name="pick",
    )(lists, table)


def embed_kernel(
    where_ref, slot_ref, code_ref, moved_ref, know_ref, extra_ref, out_ref, table_ref, *, order
):
    groups, columns, slots = moved_ref.shape
    shards, _, size = know_ref.shape

    @pl.when(pl.program_id(0) == 0)
    def _():
        for k in range(shards):
            at = pl.multiple_of((where_ref[0] ^ order[k]) * size, 128)
            table_ref[:, pl.ds(at, size)] = know_ref[k]

    slot = slot_ref[...]
    block = slot.shape[1]
    total = extra_ref[...].astype(F32)
    for n in range(groups):
        match = hot(rows_like((slots, block)) == slot - n * slots)
        total += dot_nn(moved_ref[n], match)
    for j in range(TABLES):
        match = hot(rows_like((KNOW, block)) == code_ref[j : j + 1, :])
        total += dot_nn(table_ref[:, j * KNOW : (j + 1) * KNOW], match)
    out_ref[...] = total.astype(BF)


def embed(half, turned, order, slot, codes, moved, know, extra):
    count = slot.shape[1] // 2
    columns = moved.shape[1]
    block = min(512, count)
    steps = count // block
    return pl.pallas_call(
        partial(embed_kernel, order=order),
        grid_spec=pltpu.PrefetchScalarGridSpec(
            num_scalar_prefetch=1,
            grid=(steps,),
            in_specs=[
                pl.BlockSpec((1, block), lambda i, s: (0, steps * half + i)),
                pl.BlockSpec((TABLES, block), lambda i, s: (0, steps * half + i)),
                whole(moved.shape),
                whole(know.shape),
                pl.BlockSpec((columns, block), lambda i, s: (0, steps * half + i)),
            ],
            out_specs=pl.BlockSpec((columns, block), lambda i, s: (0, i)),
            scratch_shapes=[pltpu.VMEM((columns, TABLES * KNOW), BF)],
        ),
        out_shape=shape((columns, count), BF),
        compiler_params=params(),
        cost_estimate=cost(6),
        name="embed",
    )(turned[None], slot, codes, moved, know, extra)


def more_kernel(slot_ref, moved_ref, have_ref, out_ref):
    groups, columns, slots = moved_ref.shape
    slot = slot_ref[...]
    block = slot.shape[1]
    total = have_ref[...].astype(F32)
    for n in range(groups):
        match = hot(rows_like((slots, block)) == slot - n * slots)
        total += dot_nn(moved_ref[n], match)
    out_ref[...] = total.astype(BF)


def embed_more(slot, moved, have):
    columns, count = have.shape
    block = min(512, count)
    return pl.pallas_call(
        more_kernel,
        grid=(count // block,),
        in_specs=[
            pl.BlockSpec((1, block), lambda i: (0, i)),
            pl.BlockSpec(moved.shape, lambda i: (0, 0, 0)),
            pl.BlockSpec((columns, block), lambda i: (0, i)),
        ],
        out_specs=pl.BlockSpec((columns, block), lambda i: (0, i)),
        out_shape=shape((columns, count), BF),
        compiler_params=params(),
        name="embed_more",
    )(slot, moved, have)


def bucket_kernel(slot_ref, near_ref, far_ref, out_ref):
    slots = out_ref.shape[2]
    half = near_ref.shape[1]
    start = pl.program_id(0) * slots
    match = hot(rows_like((slots, 2 * half)) == slot_ref[...] - start)
    total = dot_nt(near_ref[...], match[:, :half]) + dot_nt(far_ref[...], match[:, half:])
    out_ref[0] = total.astype(BF)


def bucket(slot, near, far, groups, slots):
    columns = near.shape[0]
    return pl.pallas_call(
        bucket_kernel,
        grid=(groups,),
        in_specs=[whole(slot.shape), whole(near.shape), whole(far.shape)],
        out_specs=pl.BlockSpec((1, columns, slots), lambda i: (i, 0, 0)),
        out_shape=shape((groups, columns, slots), BF),
        compiler_params=params(),
        cost_estimate=cost(0.2),
        name="bucket",
    )(slot, near, far)


def know_grad_kernel(where_ref, code_ref, *refs, base, parts):
    out_ref = refs[-1]
    size = out_ref.shape[2]
    count = code_ref.shape[1]
    step = pl.program_id(0)
    start = (where_ref[0] ^ (base + 4 * (step % 2) + step // 2)) * size
    first = start // KNOW
    last = (start + size - 1) // KNOW
    rows = rows_like((size, count)) + start
    match = rows == code_ref[pl.ds(first, 1), :] + first * KNOW
    match = match | (rows == code_ref[pl.ds(last, 1), :] + last * KNOW)
    match = hot(match)
    width = count // parts
    total = sum(dot_nt(refs[k][...], match[:, k * width : (k + 1) * width]) for k in range(parts))
    if len(refs) > parts + 1:
        total += refs[parts][0].astype(F32)
    out_ref[0] = total.astype(BF)


def know_grads(turned, codes, start, data, base, have):
    columns, count = data[0].shape
    size = TABLES * KNOW // SHARDS
    part = pl.BlockSpec((1, columns, size), lambda i, s: (i, 0, 0))
    return pl.pallas_call(
        partial(know_grad_kernel, base=base, parts=len(data)),
        grid_spec=pltpu.PrefetchScalarGridSpec(
            num_scalar_prefetch=1,
            grid=(4,),
            in_specs=[pl.BlockSpec((TABLES, count * len(data)), lambda i, s: (0, start))]
            + [whole(d.shape) for d in data]
            + [part] * len(have),
            out_specs=part,
        ),
        out_shape=shape((4, columns, size), BF),
        compiler_params=params(),
        cost_estimate=cost(0.2),
        name="know_grads",
    )(turned[None], codes, *data, *have)


def collect_kernel(list_ref, sent_ref, out_ref):
    groups, columns, slots = sent_ref.shape
    block = out_ref.shape[1]
    start = pl.program_id(0) * block
    total = jnp.zeros((columns, block), F32)
    for n in range(groups):
        match = hot(lanes_like((slots, block)) == list_ref[n] - start)
        total += dot_nn(sent_ref[n], match)
    out_ref[...] = total


def collect(lists, sent, owned):
    groups, columns, slots = sent.shape
    block = 512
    return pl.pallas_call(
        collect_kernel,
        grid=(pl.cdiv(owned, block),),
        in_specs=[
            pl.BlockSpec(lists.shape, lambda i: (0, 0, 0)),
            pl.BlockSpec(sent.shape, lambda i: (0, 0, 0)),
        ],
        out_specs=pl.BlockSpec((columns, block), lambda i: (0, i)),
        out_shape=shape((columns, owned), F32),
        compiler_params=params(),
        cost_estimate=cost(15),
        name="collect",
    )(lists, sent)


def add_know_kernel(where_ref, have_ref, *refs, order, window):
    know_refs, out_ref, table_ref = refs[:-2], refs[-2], refs[-1]
    columns, size = know_refs[0].shape
    step = pl.program_id(0)

    @pl.when(step == 0)
    def _():
        for k, know_ref in enumerate(know_refs):
            table_ref[:, order[k] * size : (order[k] + 1) * size] = know_ref[...]

    block = out_ref.shape[1]
    total = len(know_refs) * size
    origin = step * block - where_ref[0]
    base = jnp.clip((origin // 128) * 128, 0, total - window)
    base = pl.multiple_of(base, 128)
    part = table_ref[:, pl.ds(base, window)].astype(F32)
    turn = lax.rem(lax.rem(base - origin, window) + window, window)
    part = pltpu.roll(part, turn, 1)[:, :block]
    index = lanes_like((columns, block)) + origin
    out_ref[...] = have_ref[...] + jnp.where((index >= 0) & (index < total), part, 0.0)


def add_know(offset, have, know, order):
    columns, owned = have.shape
    block = 1024
    part = pl.BlockSpec((columns, block), lambda i, s: (0, i))
    return pl.pallas_call(
        partial(add_know_kernel, order=order, window=block + 128),
        grid_spec=pltpu.PrefetchScalarGridSpec(
            num_scalar_prefetch=1,
            grid=(pl.cdiv(owned, block),),
            in_specs=[part] + [pl.BlockSpec(k.shape, lambda i, s: (0, 0)) for k in know],
            out_specs=part,
            scratch_shapes=[pltpu.VMEM((columns, TABLES * KNOW), BF)],
        ),
        out_shape=shape((columns, owned), F32),
        input_output_aliases={1: 0},
        compiler_params=params(),
        cost_estimate=cost(0.2),
        name="add_know",
    )(offset[None], have, *know)


def collect_more_kernel(list_ref, sent_ref, have_ref, out_ref):
    groups, columns, slots = sent_ref.shape
    block = out_ref.shape[1]
    start = pl.program_id(0) * block
    total = have_ref[...]
    for n in range(groups):
        match = hot(lanes_like((slots, block)) == list_ref[n] - start)
        total += dot_nn(sent_ref[n], match)
    out_ref[...] = total


def collect_more(lists, sent, have):
    columns, owned = have.shape
    block = 512
    return pl.pallas_call(
        collect_more_kernel,
        grid=(pl.cdiv(owned, block),),
        in_specs=[
            pl.BlockSpec(lists.shape, lambda i: (0, 0, 0)),
            pl.BlockSpec(sent.shape, lambda i: (0, 0, 0)),
            pl.BlockSpec((columns, block), lambda i: (0, i)),
        ],
        out_specs=pl.BlockSpec((columns, block), lambda i: (0, i)),
        out_shape=shape((columns, owned), F32),
        compiler_params=params(),
        name="collect_more",
    )(lists, sent, have)


def project_kernel(where_ref, e0, e1, e2, e3, vec_ref, w_ref, bias_ref, f_ref, p_ref, col_ref):
    col_ref[...] = vec_ref[...].T
    pieces = [e[...].astype(F32) for e in (e0, e1, e2, e3)]
    part = pieces[0].shape[0]
    width = 4 * part
    average = sum(jnp.sum(p, 0, keepdims=True) for p in pieces) / width
    pieces = [p - average for p in pieces]
    spread = sum(jnp.sum(p * p, 0, keepdims=True) for p in pieces) / width
    scale = lax.rsqrt(spread + norm_eps)
    for j in range(4):
        rows = pl.ds(pl.multiple_of((where_ref[0] ^ j) * part, 64), part)
        unit = pieces[j] * scale
        f_ref[rows, :] = (unit * col_ref[rows, 0:1] + col_ref[rows, 1:2]).astype(BF)
    p_ref[...] = (dot_nn(w_ref[...], f_ref[...]) + bias_ref[...].T[:, 0:1]).astype(BF)


def project(place, pieces, vectors, weight, bias):
    part, count = pieces[0].shape
    block = count // 2

    def piece_spec(j):
        return pl.BlockSpec((part, block), lambda i, s: (0, i ^ (j & 1)))

    return pl.pallas_call(
        project_kernel,
        grid_spec=pltpu.PrefetchScalarGridSpec(
            num_scalar_prefetch=1,
            grid=(2,),
            in_specs=[piece_spec(j) for j in range(4)]
            + [whole(vectors.shape), whole(weight.shape), whole(bias.shape)],
            scratch_shapes=[pltpu.VMEM((4 * part, 8), F32)],
            out_specs=[
                pl.BlockSpec((4 * part, block), lambda i, s: (0, i)),
                pl.BlockSpec((weight.shape[0], block), lambda i, s: (0, i)),
            ],
        ),
        out_shape=[shape((4 * part, count), BF), shape((weight.shape[0], count), BF)],
        compiler_params=params(),
        cost_estimate=cost(4),
        name="project",
    )(place[None], *pieces, vectors, weight, bias)


def two_parts(value):
    high = value.astype(BF).astype(F32)
    return high, value - high


def widened(part, head, head_dim, extra):
    columns, count = part.shape
    rows = rows_like((columns, count))
    keep = (rows >= head * head_dim) & (rows < (head + 1) * head_dim)
    kept = jnp.where(keep, part, 0.0)
    below = rows_like((256 - columns, count))
    rest = jnp.zeros((256 - columns, count), F32)
    for at, row in enumerate(extra):
        rest = jnp.where(below == at, row, rest)
    return jnp.concatenate([kept, rest], 0).astype(BF)


def attend_kernel(
    q_ref, near_ref, far_ref, mask_ref, out_ref, lse_ref, keys_ref, values_ref, *, heads, head_dim
):
    columns = heads * head_dim
    half = near_ref.shape[1]
    count = 2 * half

    @pl.when(pl.program_id(0) == 0)
    def _():
        rest = rows_like((256 - columns, count))
        rest = jnp.where(rest == 0, mask_ref[...], 0.0)
        for at, ref in ((0, near_ref), (half, far_ref)):
            k = ref[columns : 2 * columns, :].astype(F32)
            k = jnp.concatenate([k, rest[:, at : at + half]], 0)
            keys_ref[at : at + half, :] = k.T.astype(BF)
            values_ref[:, at : at + half] = ref[2 * columns :, :]

    queries = q_ref[...].astype(F32) * head_dim ** (-0.5)
    ones = jnp.ones((1, queries.shape[1]), F32)
    for h in range(heads):
        scores = dot_nn(keys_ref[...], widened(queries, h, head_dim, [ones]))
        highest = jnp.max(scores, 0, keepdims=True)
        expanded = jnp.exp(scores - highest)
        total = jnp.sum(expanded, 0, keepdims=True)
        rows = slice(h * head_dim, (h + 1) * head_dim)
        out_ref[rows, :] = (dot_nn(values_ref[rows, :], expanded.astype(BF)) / total).astype(BF)
        lse_ref[h : h + 1, :] = highest + jnp.log(total)


def attend(near, far, mask, half, heads, head_dim):
    count = near.shape[1]
    columns = heads * head_dim
    block = 256
    return pl.pallas_call(
        partial(attend_kernel, heads=heads, head_dim=head_dim),
        grid=(count // block,),
        in_specs=[
            pl.BlockSpec((columns, block), lambda i: (0, i)),
            whole(near.shape),
            whole(far.shape),
            whole(mask.shape),
        ],
        out_specs=[
            pl.BlockSpec((columns, block), lambda i: (0, i)),
            pl.BlockSpec((8, block), lambda i: (0, i)),
        ],
        out_shape=[shape((columns, count), BF), shape((8, count), F32)],
        scratch_shapes=[pltpu.VMEM((2 * count, 256), BF), pltpu.VMEM((columns, 2 * count), BF)],
        compiler_params=params(),
        cost_estimate=cost(16),
        name="attend",
    )((near, far)[half], near, far, mask)


def attend_back_kernel(
    near_ref, far_ref, mask_ref, o_near, o_far, g_ref, lse_near, lse_far, d_ref,
    keys_ref, values_ref, flat_ref, q_ref, o_ref, lse_ref, dk_acc, dv_acc, *, heads, head_dim,
):
    step = pl.program_id(0)
    columns = heads * head_dim
    half = near_ref.shape[1]
    count = 2 * half
    block = g_ref.shape[1]
    steps = half // block

    @pl.when(step < steps)
    def _():
        at = pl.ds(pl.multiple_of(step * block, 128), block)
        q_ref[...] = near_ref[:columns, at]
        o_ref[...] = o_near[:, at]
        lse_ref[...] = lse_near[:, at]

    @pl.when(step >= steps)
    def _():
        at = pl.ds(pl.multiple_of((step - steps) * block, 128), block)
        q_ref[...] = far_ref[:columns, at]
        o_ref[...] = o_far[:, at]
        lse_ref[...] = lse_far[:, at]

    @pl.when(step == 0)
    def _():
        rest = rows_like((256 - columns, count))
        ones = jnp.where((rest == 1) | (rest == 2), 1.0, 0.0)
        with_mask = jnp.where(rest == 0, mask_ref[...], ones)
        for at, ref in ((0, near_ref), (half, far_ref)):
            part = slice(at, at + half)
            k = ref[columns : 2 * columns, :]
            v = ref[2 * columns :, :].astype(F32)
            flat_ref[:, part] = k
            k = jnp.concatenate([k.astype(F32), with_mask[:, part]], 0)
            keys_ref[part, :] = k.T.astype(BF)
            values_ref[part, :] = jnp.concatenate([v, ones[:, part]], 0).T.astype(BF)
        dk_acc[...] = jnp.zeros_like(dk_acc)
        dv_acc[...] = jnp.zeros_like(dv_acc)

    score_scale = head_dim ** (-0.5)
    queries = q_ref[...].astype(F32) * score_scale
    grads = g_ref[...].astype(F32)
    inner = grads * o_ref[...].astype(F32)
    by_query = queries.T
    by_grad = grads.T
    lanes = lanes_like(by_query.shape)
    one = jnp.ones((1, block), F32)
    zero = jnp.zeros((1, block), F32)
    here = pl.ds(pl.multiple_of(step * block, 128), block)
    for h in range(heads):
        rows = slice(h * head_dim, (h + 1) * head_dim)
        keep = (lanes >= h * head_dim) & (lanes < (h + 1) * head_dim)
        lse = two_parts(-lse_ref[h : h + 1, :])
        delta = two_parts(-jnp.sum(inner[rows, :], 0, keepdims=True))
        scores = dot_nn(keys_ref[...], widened(queries, h, head_dim, [one, *lse]))
        probs = jnp.exp(scores)
        dv_acc[...] += dot_nn(probs.astype(BF), jnp.where(keep, by_grad, 0.0).astype(BF))
        grad_probs = dot_nn(values_ref[...], widened(grads, h, head_dim, [zero, *delta]))
        grad_scores = (probs * grad_probs).astype(BF)
        dk_acc[...] += dot_nn(grad_scores, jnp.where(keep, by_query, 0.0).astype(BF))
        d_ref[rows, here] = (dot_nn(flat_ref[rows, :], grad_scores) * score_scale).astype(BF)

    @pl.when(step == pl.num_programs(0) - 1)
    def _():
        d_ref[columns : 2 * columns, :] = dk_acc[...].T.astype(BF)
        d_ref[2 * columns :, :] = dv_acc[...].T.astype(BF)


def attend_back(near, far, mask, out, grad, lse, heads, head_dim):
    rows, half = near.shape
    count = 2 * half
    columns = heads * head_dim
    block = min(512, half)
    arrays = (near, far, mask, *out, grad, *lse)
    specs = [whole(a.shape) for a in arrays]
    specs[5] = pl.BlockSpec((columns, block), lambda i: (0, i))
    return pl.pallas_call(
        partial(attend_back_kernel, heads=heads, head_dim=head_dim),
        grid=(count // block,),
        in_specs=specs,
        out_specs=whole((rows, count)),
        out_shape=shape((rows, count), BF),
        scratch_shapes=[
            pltpu.VMEM((count, 256), BF),
            pltpu.VMEM((count, 256), BF),
            pltpu.VMEM((columns, count), BF),
            pltpu.VMEM((columns, block), BF),
            pltpu.VMEM((columns, block), BF),
            pltpu.VMEM((8, block), F32),
            pltpu.VMEM((count, columns), F32),
            pltpu.VMEM((count, columns), F32),
        ],
        compiler_params=params(),
        cost_estimate=cost(38),
        name="attend_back",
    )(*arrays)


def to_second_kernel(where_ref, *refs):
    h_refs, e_refs, o_refs = refs[0:4], refs[4:8], refs[8:12]
    vec_ref, resid_ref, upper_ref, lower_ref, emb_ref = refs[12:]
    part = h_refs[0].shape[0]
    for j in range(4):
        rows = pl.ds(pl.multiple_of((where_ref[0] ^ j) * part, 64), part)
        emb_ref[rows, :] = e_refs[j][...].astype(F32)
    resid = emb_ref[...].T + vec_ref[0:1, :]
    for j in range(4):
        resid += dot_tn(h_refs[j][...], o_refs[j][...])
    resid_ref[...] = resid
    centered = resid - jnp.mean(resid, -1, keepdims=True)
    spread = jnp.mean(centered * centered, -1, keepdims=True)
    unit = centered * lax.rsqrt(spread + norm_eps)
    second = (unit * vec_ref[1:2, :] + vec_ref[2:3, :]).astype(BF)
    half = second.shape[0] // 2
    upper_ref[...] = second[:half]
    lower_ref[...] = second[half:]


def to_second(place, heads, pieces, outs, vectors):
    part, count = heads[0].shape
    width = outs[0].shape[1]

    def piece_spec(j):
        return pl.BlockSpec((part, count), lambda i, s: (0, j & 1))

    return pl.pallas_call(
        to_second_kernel,
        grid_spec=pltpu.PrefetchScalarGridSpec(
            num_scalar_prefetch=1,
            grid=(1,),
            in_specs=[whole((part, count))] * 4
            + [piece_spec(j) for j in range(4)]
            + [whole(w.shape) for w in outs]
            + [whole(vectors.shape)],
            out_specs=[whole((count, width))] + [whole((count // 2, width))] * 2,
            scratch_shapes=[pltpu.VMEM((width, count), F32)],
        ),
        out_shape=[shape((count, width), F32)] + [shape((count // 2, width), BF)] * 2,
        compiler_params=params(),
        cost_estimate=cost(4),
        name="to_second",
    )(place[None], *heads, *pieces, *outs, vectors)


def feed_kernel(s0, s1, g0, g1, up_ref, down_ref, bias_ref, *outs):
    for k, (second_ref, g_ref) in enumerate(((s0, g0), (s1, g1))):
        act_ref, pre_ref, grad_ref = outs[3 * k : 3 * k + 3]
        pre_act = dot_nn(second_ref[...], up_ref[...]) + bias_ref[...]
        inside = 0.5 * (1.0 + lax.erf(pre_act * (0.5**0.5)))
        density = jnp.exp(-0.5 * pre_act * pre_act) * 0.3989422804014327
        act_ref[...] = (pre_act * inside).astype(BF)
        grad_act = dot_nt(g_ref[...], down_ref[...])
        grad_pre = (grad_act * (inside + pre_act * density)).astype(BF)
        pre_ref[...] = grad_pre
        grad_ref[...] = dot_nt(grad_pre, up_ref[...]).astype(BF)


def feed_pair(seconds, grad_outs, up, down, bias):
    count, width = seconds[0].shape
    units = up.shape[1]
    arrays = (*seconds, *grad_outs, up, down, bias)
    unit, token = shape((count, units), BF), shape((count, width), BF)
    found = pl.pallas_call(
        feed_kernel,
        grid=(1,),
        in_specs=[whole(a.shape) for a in arrays],
        out_specs=[whole(a.shape) for a in (unit, unit, token) * 2],
        out_shape=[unit, unit, token] * 2,
        compiler_params=params(),
        cost_estimate=cost(5),
        name="feed_pair",
    )(*arrays)
    return found[:3], found[3:]


def rows_of(refs):
    return jnp.concatenate([r[...] for r in refs], 0)


def feed_weight_kernel(*refs):
    s_refs, p_refs, a_refs, g_refs = refs[0:8], refs[8:16], refs[16:24], refs[24:32]
    out_ref, sum_ref = refs[32:]
    up = dot_tn(rows_of(s_refs), rows_of(p_refs))
    out_ref[0] = up.astype(BF)
    down = dot_tn(rows_of(a_refs), rows_of(g_refs))
    out_ref[1] = down.astype(BF)
    total = sum(jnp.sum(p[...].astype(F32), 0, keepdims=True) for p in p_refs)
    sum_ref[...] = jnp.broadcast_to(total, sum_ref.shape)


def feed_weights(seconds, grad_pres, activated, grad_outs):
    width, units = seconds[0].shape[1], grad_pres[0].shape[1]
    arrays = (*seconds, *grad_pres, *activated, *grad_outs)
    return pl.pallas_call(
        feed_weight_kernel,
        grid=(1,),
        in_specs=[whole(a.shape) for a in arrays],
        out_specs=[whole((2, width, units)), whole((8, units))],
        out_shape=[shape((2, width, units), BF), shape((8, units), F32)],
        compiler_params=params(),
        cost_estimate=cost(9),
        name="feed_weights",
    )(*arrays)


def to_heads_kernel(resid_ref, a0, a1, b0, b1, c0, c1, g0, g1, *refs):
    o_refs = refs[0:4]
    vec_ref, low_ref, grad_ref, heads_ref, sums_ref = refs[4:]
    resid = resid_ref[...]
    centered = resid - jnp.mean(resid, -1, keepdims=True)
    spread = jnp.mean(centered * centered, -1, keepdims=True)
    scale = lax.rsqrt(spread + norm_eps)
    unit = centered * scale
    grad_second = sum(rows_of(pair).astype(F32) for pair in ((a0, a1), (b0, b1), (c0, c1)))
    e = grad_second * vec_ref[1:2, :]
    first_mean = jnp.mean(e, -1, keepdims=True)
    second_mean = jnp.mean(e * unit, -1, keepdims=True)
    grad_out = rows_of((g0, g1)).astype(F32)
    grad_resid = grad_out + scale * (e - first_mean - unit * second_mean)
    low = grad_resid.astype(BF)
    low_ref[...] = low
    grad_ref[...] = grad_resid.T
    for j in range(4):
        heads_ref[j] = dot_nt(o_refs[j][...], low).astype(BF)
    rows = [grad_second * unit, grad_second, grad_resid, grad_out]
    rows = [jnp.sum(r, 0, keepdims=True) for r in rows]
    blank = jnp.zeros_like(rows[0])

    sums_ref[...] = jnp.concatenate(rows + [blank] * 4, 0)


def to_heads(resid, terms, grad_outs, outs, vectors):
    count, width = resid.shape
    part = outs[0].shape[0]
    token = whole((count, width))
    arrays = (resid, *terms, *grad_outs, *outs, vectors)
    return pl.pallas_call(
        to_heads_kernel,
        grid=(1,),
        in_specs=[whole(a.shape) for a in arrays],
        out_specs=[token, whole((width, count)), whole((4, part, count)), whole((8, width))],
        out_shape=[
            shape((count, width), BF),
            shape((width, count), F32),
            shape((4, part, count), BF),
            shape((8, width), F32),
        ],
        compiler_params=params(),
        cost_estimate=cost(6),
        name="to_heads",
    )(*arrays)


def rest_kernel(near_ref, far_ref, l0, l1, l2, l3, back_ref, f_near, f_far, out_ref):
    columns, half = near_ref.shape
    quarter = half // 2
    total = dot_nn(near_ref[:, :quarter], l0[...]) + dot_nn(near_ref[:, quarter:], l1[...])
    total += dot_nn(far_ref[:, :quarter], l2[...]) + dot_nn(far_ref[:, quarter:], l3[...])
    out_ref[:columns, :] = total.astype(BF)
    total = dot_nt(back_ref[:, :half], f_near[...]) + dot_nt(back_ref[:, half:], f_far[...])
    out_ref[columns:, :] = total.astype(BF)


def rest_weights(near, far, lows, back, firsts):
    width = firsts[0].shape[0]
    arrays = (near, far, *lows, back, *firsts)
    dims = (near.shape[0] + back.shape[0], width)
    return pl.pallas_call(
        rest_kernel,
        grid=(1,),
        in_specs=[whole(a.shape) for a in arrays],
        out_specs=whole(dims),
        out_shape=shape(dims, BF),
        compiler_params=params(),
        cost_estimate=cost(6),
        name="rest_weights",
    )(*arrays)


def back_kernel(back_ref, w_ref, *outs):
    for j, out_ref in enumerate(outs):
        count = out_ref.shape[1]
        rows = back_ref[:, j * count : (j + 1) * count]
        out_ref[...] = dot_nn(w_ref[...], rows).astype(BF)


def first_grads(back, weight):
    count = back.shape[1] // 4
    width = weight.shape[0]
    return pl.pallas_call(
        back_kernel,
        grid=(1,),
        in_specs=[whole(back.shape), whole(weight.shape)],
        out_specs=[whole((width, count))] * 4,
        out_shape=[shape((width, count), BF)] * 4,
        compiler_params=params(),
        cost_estimate=cost(3),
        name="first_grads",
    )(back, weight)


def finish_kernel(
    where_ref, a_ref, b_ref, c_ref, e0, e1, e2, e3, resid_ref, vec_ref,
    cols_ref, rows_ref, sums_ref, emb_ref,
):
    part = e0.shape[0]
    width = 4 * part
    for j, e in enumerate((e0, e1, e2, e3)):
        rows = pl.ds(pl.multiple_of((where_ref[0] ^ j) * part, 64), part)
        emb_ref[rows, :] = e[...].astype(F32)
    grad = a_ref[...].astype(F32) + b_ref[...].astype(F32) + c_ref[...].astype(F32)
    values = emb_ref[...]
    centered = values - jnp.sum(values, 0, keepdims=True) / width
    spread = jnp.sum(centered * centered, 0, keepdims=True) / width
    scale = lax.rsqrt(spread + norm_eps)
    unit = centered * scale
    e = grad * vec_ref[...].T[:, 0:1]
    first_mean = jnp.sum(e, 0, keepdims=True) / width
    second_mean = jnp.sum(e * unit, 0, keepdims=True) / width
    total = resid_ref[...] + scale * (e - first_mean - unit * second_mean)
    emb_ref[...] = total
    for j in range(4):
        rows = pl.ds(pl.multiple_of((where_ref[0] ^ j) * part, 64), part)
        cols_ref[j] = emb_ref[rows, :].astype(BF)
    rows_ref[...] = total.T.astype(BF)
    sums_ref[:, 0:1] = jnp.sum(grad * unit, 1, keepdims=True)
    sums_ref[:, 1:2] = jnp.sum(grad, 1, keepdims=True)


def finish(place, a, b, c, pieces, resid, vectors):
    width, count = a.shape
    part = pieces[0].shape[0]

    def piece_spec(j):
        return pl.BlockSpec((part, count), lambda i, s: (0, j & 1))

    return pl.pallas_call(
        finish_kernel,
        grid_spec=pltpu.PrefetchScalarGridSpec(
            num_scalar_prefetch=1,
            grid=(1,),
            in_specs=[whole(a.shape)] * 3
            + [piece_spec(j) for j in range(4)]
            + [whole(resid.shape), whole(vectors.shape)],
            out_specs=[whole((4, part, count)), whole((count, width)), whole((width, 128))],
            scratch_shapes=[pltpu.VMEM((width, count), F32)],
        ),
        out_shape=[
            shape((4, part, count), BF),
            shape((count, width), BF),
            shape((width, 128), F32),
        ],
        compiler_params=params(),
        cost_estimate=cost(4),
        name="finish",
    )(place[None], a, b, c, *pieces, resid, vectors)


def body(
    gene_ids,
    know_ids,
    lengths,
    tables,
    norm_gain,
    norm_bias,
    qkv_weight,
    qv_bias,
    out_weight,
    out_bias,
    up_weight,
    up_bias,
    down_weight,
    down_bias,
    cotangent,
):
    count = gene_ids.shape[0]
    width = norm_gain.shape[1]
    columns = qkv_weight.shape[2]
    units = up_weight.shape[1]
    head_dim = width // HEADS
    heads_here = columns // head_dim
    owned = tables.shape[0]
    groups = lax.axis_size("dp")
    place = lax.axis_index("tensor")
    group = lax.axis_index("dp")
    quarter = count // 4
    length = lengths[0]
    slots = 128 * (-(-(3 * count // (2 * groups)) // 128))
    know_rows = TABLES * KNOW
    share = know_rows // SHARDS
    start = VOCAB - (groups - 1) * owned
    one_owner = start >= 0 and groups == SHARDS

    def block_at(value, j, size, axis=0):
        return lax.dynamic_slice_in_dim(value, (place ^ j) * size, size, axis)

    def relative(value, size, axis=0):
        return jnp.concatenate([block_at(value, j, size, axis) for j in range(4)], axis)

    ids = relative(gene_ids, quarter)[None]
    codes = relative(know_ids, quarter, 1)
    step = 1
    while step < groups:
        ids = jnp.concatenate([ids, hop(ids, "dp", step)], 0)
        step *= 2
    lists, slot, most = route(group, jnp.int32(0), ids, owned, slots)
    rounds = (most[0, 0] + slots - 1) // slots

    table = tables.T

    picked = pick(lists, table)

    if one_owner:
        held = after(table, ids)[:, start : start + know_rows]
        shards = [held[:, i * share : (i + 1) * share] for i in range(SHARDS)]
        dealt = [lax.ppermute(shards[i], "dp", [(groups - 1, i)]) for i in range(groups - 1)]
        mine = jnp.where(group == groups - 1, shards[-1], jnp.zeros((), BF))
        mine = sum(after(dealt, picked), mine)
        know, order = mine[None], (0,)
        for step in (4, 2, 1):
            know = jnp.concatenate([know, hop(know, "dp", step)], 0)
            order = order + tuple(k | step for k in order)
        turned = group
    else:
        room = jnp.pad(table, ((0, 0), (know_rows, know_rows)))
        begin = jnp.clip(VOCAB - group * owned + know_rows, 0, owned + know_rows)
        know = lax.psum(lax.dynamic_slice_in_dim(room, begin, know_rows, 1), "dp")
        know = jnp.stack([know[:, i * share : (i + 1) * share] for i in range(SHARDS)])
        turned = jnp.int32(0)
        order = tuple(range(SHARDS))

    def exchange(blocks):
        return lax.all_to_all(blocks, "dp", 0, 0, tiled=True)

    def more_rows(carry):
        turn, total = carry
        these, at, _ = route(group, turn, ids, owned, slots)
        return turn + 1, embed_more(at, exchange(pick(these, table)), total)

    blank = jnp.zeros((columns, count), BF)
    _, extra = lax.while_loop(lambda c: c[0] < rounds, more_rows, (jnp.int32(1), blank))

    out_blocks = gather_four(out_weight)
    moved = exchange(picked)
    moved = after(moved, extra, *out_blocks)

    own = [embed(0, turned, order, slot, codes, moved, know, extra)]
    far = [hop(own[0], "tensor", 2)]
    own.append(embed(1, turned, order, slot, codes, after(moved, own[0]), know, extra))
    far.append(hop(after(own[1], far[0]), "tensor", 2))
    near = [hop(o, "tensor", 1) for o in own]
    third = [hop(far[0], "tensor", 1)]

    gain = norm_gain.astype(F32)
    shift = norm_bias.astype(F32)
    weight = qkv_weight.transpose(0, 2, 1).reshape(3 * columns, width)
    weight_down = weight.T
    bias = qv_bias.astype(F32)
    bias = jnp.concatenate([bias[0], jnp.zeros((columns,), F32), bias[1]])[None]
    bias = jnp.pad(bias, ((0, 7), (0, 0)))
    norm_rows = jnp.pad(jnp.stack([gain[0], shift[0]]), ((0, 6), (0, 0)))
    upper = (own[1], near[1], far[0], third[0])
    upper = project(place, upper, norm_rows, weight, bias)
    far[1] = after(far[1], upper)
    third.append(hop(far[1], "tensor", 1))
    lower = (own[0], near[0], far[1], third[1])
    halves = project(place, lower, norm_rows, weight, bias), upper
    pieces = (own[0], near[0], far[1], third[1])
    firsts, projected = zip(*halves)
    spots = relative(jnp.arange(count, dtype=I32), quarter)
    mask = jnp.where(spots < length, 0.0, -1e30).astype(F32)[None]
    valid = jnp.arange(count, dtype=I32) < length
    grad_full = cotangent * valid[:, None].astype(BF)
    eighth = quarter // 2
    grad_outs = []
    for j in range(4):
        rows = block_at(grad_full, j, quarter)
        grad_outs.append((rows[:eighth], rows[eighth:]))
    far_heads, far_lse = attend(*projected, after(mask, grad_outs, weight_down), 1, heads_here, head_dim)
    near_heads, near_lse = attend(*projected, after(mask, far_heads), 0, heads_here, head_dim)

    from_far = [hop(far_heads[:, k * quarter :][:, :quarter], "tensor", 2 + k) for k in (0, 1)]
    near_heads = after(near_heads, from_far)
    heads = [near_heads[:, :quarter], hop(near_heads[:, quarter:], "tensor", 1), *from_far]
    vectors = jnp.stack([out_bias.astype(F32), gain[1], shift[1]])
    up_row = up_bias.astype(F32)[None]

    def feed(rows, grads):
        return feed_pair(rows, grads, up_weight, down_weight, up_row)

    resid, *second = to_second(place, heads, pieces, out_blocks, vectors)
    beside = [hop(s, "tensor", 1) for s in second]
    across = [hop(s, "tensor", 2) for s in second]
    own_blocks = feed(second, grad_outs[0])
    near_blocks = feed(beside, grad_outs[1])
    blocks = [own_blocks, near_blocks]
    seconds, terms = [second, beside], []
    for half in (0, 1):
        rows = after(across[half], blocks)
        rows = [rows, hop(rows, "tensor", 1)]
        found = feed(rows, (grad_outs[2][half], grad_outs[3][half]))
        two = (found[0][2].astype(F32) + hop(found[1][2], "tensor", 1).astype(F32)).astype(BF)
        if half:
            two = after(two, terms[0])
        terms.append(hop(two, "tensor", 2))
        seconds.append(rows)
        blocks.append(found)
    pairs = [grad_outs[0], grad_outs[1]]
    pairs += [(grad_outs[2][k], grad_outs[3][k]) for k in (0, 1)]
    flat = [block for found in blocks for block in found]
    feed_part, unit_sums = feed_weights(
        [rows for pair in seconds for rows in pair],
        [f[1] for f in flat],
        [f[0] for f in flat],
        after([g for pair in pairs for g in pair], two),
    )
    low, grad_resid, grad_heads, sums = to_heads(
        resid,
        after(
            (
                *[f[2] for f in own_blocks],
                *[hop(f[2], "tensor", 1) for f in near_blocks],
                *terms,
            ),
            feed_part,
        ),
        grad_outs[0],
        out_blocks,
        vectors,
    )
    grads = jnp.concatenate(swap_four([grad_heads[j] for j in range(4)]), 1)
    low = after(low, grads)
    lows = swap_four([low] * 4)
    back = attend_back(
        *projected,
        mask,
        (near_heads, far_heads),
        grads,
        (near_lse, far_lse),
        heads_here,
        head_dim,
    )

    def sum_four(parts):
        two = parts[2].astype(F32) + hop(parts[3], "tensor", 1).astype(F32)
        zero = parts[0].astype(F32) + hop(parts[1], "tensor", 1).astype(F32)
        return zero + hop(two.astype(BF), "tensor", 2).astype(F32)

    feed_grad = lax.psum(feed_part, "dp")

    back = after(back, *lows)

    first_grad = first_grads(back, weight_down)

    two = first_grad[2].astype(F32) + hop(first_grad[3], "tensor", 1).astype(F32)
    back_later = after(back, two)
    rest = rest_weights(near_heads, far_heads, lows, back_later, firsts)
    acts = [own_blocks, near_blocks] + [[blocks[2][k], blocks[3][k]] for k in (0, 1)]
    feeds = []
    for pair in acts:
        rows = jnp.concatenate([found[0] for found in pair], 0)
        feeds.append(dot_nn(after(rows, rest), down_weight).astype(BF))
    from_far = hop(two.astype(BF), "tensor", 2)
    from_near = hop(first_grad[1], "tensor", 1)
    by_column, by_row, first_sums = finish(
        place,
        first_grad[0],
        from_near,
        from_far,
        pieces,
        grad_resid,
        norm_rows,
    )
    swapped = swap_four([by_column[j] for j in range(4)])
    near_columns = jnp.concatenate(swapped[:2], 1)
    far_columns = jnp.concatenate(swapped[2:], 1)

    odd_part = know_grads(turned, codes, 0, [near_columns], 2, ())
    far_columns = after(far_columns, odd_part)
    dealt = bucket(slot, near_columns, far_columns, groups, slots)
    sent = exchange(dealt)
    odd_part = know_grads(turned, after(codes, dealt), 1, [far_columns], 2, (odd_part,))
    both = [near_columns, far_columns]
    even_part = know_grads(turned, after(codes, odd_part, feed_grad), 0, both, 0, ())

    def halve(part):
        return part[:2].astype(F32), hop(part[2:], "dp", 1)

    if one_owner:
        odd_own, odd_other = halve(odd_part)
        odd_sum = (odd_own + odd_other.astype(F32)).astype(BF)
        even_own, even_other = halve(even_part)
        rest = lax.psum(rest, "dp", axis_index_groups=[list(range(groups))[::-1]])
        odd_far = hop(after(odd_sum, sent), "dp", 2)
    else:
        rest = lax.psum(after(rest, feed_grad), "dp")
    downs = after(lists, firsts).transpose(0, 2, 1)
    tables_grad = collect(downs, sent, owned)
    if one_owner:
        even_sum = even_own + even_other.astype(F32) + odd_far.astype(F32)
        know_sum = even_sum[0] + hop(even_sum[1].astype(BF), "dp", 4).astype(F32)
        know_sum = after(know_sum.astype(BF), tables_grad)
        last = jnp.where(group == groups - 1, know_sum, jnp.zeros((), BF))
        know_all = [lax.ppermute(know_sum, "dp", [(i, groups - 1)]) for i in range(groups - 1)]
        know_all, order = know_all + [last], tuple(range(SHARDS))
    else:
        know_all = lax.psum(jnp.concatenate([even_part, odd_part], 0), "dp")
        know_sum = know_all
        know_all, order = [know_all[k] for k in range(SHARDS)], (0, 4, 1, 5, 2, 6, 3, 7)

    def more_grads(carry):
        turn, total = carry
        these, at, _ = route(group, turn, ids, owned, slots)
        these = these.transpose(0, 2, 1)
        return turn + 1, collect_more(
            these, exchange(bucket(at, near_columns, far_columns, groups, slots)), total
        )

    _, tables_grad = lax.while_loop(
        lambda c: c[0] < rounds, more_grads, (jnp.int32(1), tables_grad)
    )

    feeds = after(feeds, far_columns)
    out_own = (resid + sum_four(feeds) + down_bias.astype(F32)).astype(BF)

    def spread_rows(own, kind):
        full = jnp.zeros((count, width), kind)
        for j, block in enumerate(gather_four(own)):
            full = lax.dynamic_update_slice_in_dim(
                full, block.astype(kind), (place ^ j) * quarter, 0
            )
        return full

    out = spread_rows(after(out_own, far_columns), BF)
    input_grad = spread_rows(after(by_row, far_columns), F32)

    feed_grad = after(feed_grad, sent).astype(F32)

    qv = jnp.sum(back.reshape(3, columns, count).astype(F32), -1)
    qv = jnp.stack([qv[0], qv[2]])
    qv_wide = lax.dynamic_update_slice_in_dim(
        jnp.zeros((2, width), F32), qv, place * columns, 1
    )
    up_sums = lax.dynamic_update_slice_in_dim(
        jnp.zeros((4, units), F32), unit_sums[0:1], place, 0
    )
    packed = jnp.concatenate(
        [
            first_sums[:, 0],
            first_sums[:, 1],
            sums[0:4].reshape(-1),
            qv_wide.reshape(-1),
            up_sums.reshape(-1),
        ]
    ).reshape(-1, 128)
    packed = after(packed, know_sum)
    for step in (1, 2):
        packed = packed + hop(packed, "tensor", step)
    step = 1
    while step < groups:
        packed = packed + hop(packed, "dp", step)
        step *= 2
    packed = packed.reshape(-1)
    know_all = after(know_all, packed, out, input_grad, feed_grad, rest)
    tables_grad = add_know(VOCAB - group * owned, tables_grad, know_all, order)
    rest = after(rest, tables_grad).astype(F32)
    outw_grad = rest[:columns]
    qkv_grad = rest[columns:].reshape(3, columns, width).transpose(0, 2, 1)
    tops = packed[: 6 * width].reshape(6, width)
    qv_wide = packed[6 * width : 8 * width].reshape(2, width)
    up_sums = packed[8 * width :].reshape(4, units)
    return (
        out,
        input_grad,
        tables_grad.T,
        jnp.stack([tops[0], tops[2]]),
        jnp.stack([tops[1], tops[3]]),
        qkv_grad,
        lax.dynamic_slice_in_dim(qv_wide, place * columns, columns, 1),
        outw_grad,
        tops[4],
        feed_grad[0],
        lax.dynamic_slice_in_dim(up_sums, place, 1, 0)[0],
        feed_grad[1],
        tops[5],
    )


def solution(mesh):
    placed = (
        P("dp"),
        P(None, "dp"),
        P("dp"),
        P("dp", "tensor"),
        P(),
        P(),
        P(None, None, "tensor"),
        P(None, "tensor"),
        P("tensor", None),
        P(),
        P(None, "tensor"),
        P("tensor"),
        P("tensor", None),
        P(),
        P("dp", None),
    )
    return jax.shard_map(
        body,
        mesh=mesh,
        in_specs=placed,
        out_specs=(
            P("dp", None),
            P("dp", None),
            P("dp", "tensor"),
            P(),
            P(),
            P(None, None, "tensor"),
            P(None, "tensor"),
            P("tensor", None),
            P(),
            P(None, "tensor"),
            P("tensor"),
            P("tensor", None),
            P(),
        ),
        check_vma=False,
    )
```
